128 devices in a mesh: tok: 16 (over z_lo, x, core), var: 8 (over z_hi, y).
Axes of the slice: x: 4, y: 4, z: 4 (z_hi: 2, z_lo: 2; z = z_hi * 2 + z_lo), core: 2. Of those that a mesh axis runs over, the one named last changes fastest.
Arguments:
- fields: bfloat16 [48, 6144, 1024], P('var', 'tok'), may hold values from -6 to 6
- var_embed: bfloat16 [48, 1024], replicated, may hold values from -3 to 3
- pos_embed: bfloat16 [6144, 1024], P('tok'), may hold values from -3 to 3
- agg_key: bfloat16 [1024, 1024], replicated, may hold values from -0.1875 to 0.1875
- agg_query: float32 [16, 64], replicated, may hold values from -600 to 600
- agg_value: bfloat16 [1024, 1024], replicated, may hold values from -0.1875 to 0.1875
- agg_out: bfloat16 [1024, 1024], replicated, may hold values from -0.1875 to 0.1875
- gain_one: float32 [1024], replicated, may hold values from 0.1 to 1.9
- qkv_weight: bfloat16 [3, 1024, 1024], P(None, None, 'var'), may hold values from -1 to 1
- attn_out: bfloat16 [1024, 1024], P('var'), may hold values from -0.1875 to 0.1875
- gain_two: float32 [1024], replicated, may hold values from 0.1 to 1.9
- mlp_in: bfloat16 [1024, 4096], P(None, 'var'), may hold values from -0.1875 to 0.1875
- mlp_out: bfloat16 [4096, 1024], P('var'), may hold values from -0.09375 to 0.09375
Outputs:
- encoded: bfloat16 [6144, 1024], P('tok', 'var')
The draws below stay inside these ranges and needn't reach their ends.
All inputs are finite; a program needn't handle non-finite values.
Results may differ from the reference program's by a relative error of at most 0.029.
Values may be sent and summed in bfloat16 or wider, within the bound.
A program may use at most 128 MiB of HBM per device.

```python
import math
import jax
import jax.numpy as jnp
from jax import lax

D = 1024
H = 16
FF = 4096
HD = 64
VARIABLES = 48
TOKENS = 6144
N_VAR = 8


def draw_agg_query(key, part):
    key = jax.random.fold_in(key, 11)
    base = jax.random.truncated_normal(jax.random.fold_in(key, 1), -4.0, 4.0, (H, HD), jnp.float32)
    return base


def draw_qkv_weight(key, part):
    key = jax.random.fold_in(key, 12)
    base = jax.random.truncated_normal(jax.random.fold_in(key, 1), -4.0, 4.0, (3, D, D), jnp.float32) / math.sqrt(D)
    return base.astype(jnp.bfloat16)


def block_levels(key, dims, pieces, low, top_value):
    factor_of = 1.0
    for position, blocks in pieces:
        steps = jax.random.uniform(jax.random.fold_in(jax.random.fold_in(key, 6), position), (blocks,), jnp.float32, low / len(pieces), top_value / len(pieces))
        factor_of = factor_of * jnp.repeat(jnp.exp(steps), dims[position] // blocks).reshape((-1,) + (1,) * (len(dims) - 1 - position))
    return factor_of


def gaussian(own_key, extent, scale, most, cuts=(), dtype=jnp.bfloat16):
    level = block_levels(own_key, extent, cuts, -0.22, 0.18) if cuts else 1.0
    values = jax.random.normal(own_key, extent, jnp.float32) * scale * level
    return jnp.minimum(jnp.maximum(values, -most), most).astype(dtype)


def setup_inputs(seed: int = 0) -> dict:
    key_list = jax.random.split(jax.random.key(seed), 14)
    return {
        "fields": gaussian(key_list[0], (VARIABLES, TOKENS, D), 1.0, 6.0, ((0, 8), (1, 16))),
        "var_embed": gaussian(key_list[1], (VARIABLES, D), 0.5, 3.0),
        "pos_embed": gaussian(key_list[2], (TOKENS, D), 0.5, 3.0, ((0, 16),)),
        "agg_key": gaussian(key_list[3], (D, D), D ** -0.5, 0.1875),
        "agg_query": draw_agg_query(jax.random.fold_in(key_list[13], 71), 0),
        "agg_value": gaussian(key_list[5], (D, D), D ** -0.5, 0.1875),
        "agg_out": gaussian(key_list[6], (D, D), D ** -0.5, 0.1875),
        "gain_one": jnp.clip(1.0 + 0.18 * jax.random.normal(key_list[7], (D,), jnp.float32), 0.1, 1.9),
        "qkv_weight": draw_qkv_weight(jax.random.fold_in(key_list[13], 71), 0),
        "attn_out": gaussian(key_list[9], (D, D), D ** -0.5, 0.1875, ((0, 8),)),
        "gain_two": jnp.clip(1.0 + 0.18 * jax.random.normal(key_list[10], (D,), jnp.float32), 0.1, 1.9),
        "mlp_in": gaussian(key_list[11], (D, FF), D ** -0.5, 0.1875, ((1, 8),)),
        "mlp_out": gaussian(key_list[12], (FF, D), FF ** -0.5, 0.09375, ((0, 8),)),
    }


EPS = 1e-05

def layer_norm(stream, gain):
    values = stream.astype(jnp.float32)
    center = values - lax.optimization_barrier(jnp.mean(values, axis=-1, keepdims=True))
    spread = lax.optimization_barrier(jnp.mean(center * center, axis=-1, keepdims=True))
    return (center * lax.rsqrt(spread + EPS) * gain).astype(jnp.bfloat16)

def folded_query(agg_key, agg_query):
    width = agg_key.shape[0]
    heads = agg_query.shape[0]
    head_dim = agg_query.shape[1]
    keyed = agg_key.astype(jnp.float32).reshape(width, heads, head_dim)
    folded = jnp.einsum('dhe,he->dh', keyed, agg_query, precision=lax.Precision.HIGHEST)
    return (folded / math.sqrt(head_dim)).astype(jnp.bfloat16)

def weighted_values(embedded, weights, agg_value, heads):
    rows = embedded.shape[1]
    width = embedded.shape[2]

    def step(total, item):
        field, weight = item
        projected = jnp.dot(field, agg_value, preferred_element_type=jnp.float32).reshape(rows, heads, width // heads)
        return (total + (weight[:, :, None] * projected).reshape(rows, width), None)
    return lax.scan(step, jnp.zeros((rows, width), jnp.float32), (embedded, weights))[0]

def grouped_values(embedded, weights, agg_value, heads, groups):
    count = embedded.shape[0]
    rows = embedded.shape[1]
    width = embedded.shape[2]
    per_group = count // groups

    def step(total, item):
        partial_value = weighted_values(item[0], item[1], agg_value, heads).astype(jnp.bfloat16)
        partial_value = lax.optimization_barrier(partial_value)
        return (total + partial_value.astype(jnp.float32), None)
    blocks = (embedded.reshape(groups, per_group, rows, width), weights.reshape(groups, per_group, rows, heads))
    return lax.scan(step, jnp.zeros((rows, width), jnp.float32), blocks)[0]

def group_sum(left, right, groups):
    span = left.shape[1] // groups
    total = jnp.zeros((left.shape[0], right.shape[1]), jnp.float32)
    for group in range(groups):
        term = jnp.dot(left[:, group * span:(group + 1) * span], right[group * span:(group + 1) * span], preferred_element_type=jnp.float32)
        term = lax.optimization_barrier(term.astype(jnp.bfloat16))
        total = total + term.astype(jnp.float32)
    return total

def reference(fields, var_embed, pos_embed, agg_key, agg_query, agg_value, agg_out, gain_one, qkv_weight, attn_out, gain_two, mlp_in, mlp_out):
    heads = agg_query.shape[0]
    head_dim = agg_query.shape[1]
    tokens = fields.shape[1]
    width = fields.shape[2]
    key_query = folded_query(agg_key, agg_query)
    embedded = (fields.astype(jnp.float32) + var_embed.astype(jnp.float32)[:, None, :]).astype(jnp.bfloat16)
    scores = jnp.einsum('vtd,dh->vth', embedded, key_query, preferred_element_type=jnp.float32)
    expd = jnp.exp(scores - lax.optimization_barrier(jnp.max(scores, axis=0)))
    weights = expd / lax.optimization_barrier(jnp.sum(expd, axis=0))
    mixed = grouped_values(embedded, weights, agg_value, heads, N_VAR).astype(jnp.bfloat16)
    stream = (jnp.dot(mixed, agg_out, preferred_element_type=jnp.float32) + pos_embed.astype(jnp.float32)).astype(jnp.bfloat16)
    normed = layer_norm(stream, gain_one)
    query = jnp.dot(normed, qkv_weight[0], preferred_element_type=jnp.float32).astype(jnp.bfloat16)
    keys = jnp.dot(normed, qkv_weight[1], preferred_element_type=jnp.float32).astype(jnp.bfloat16)
    values = jnp.dot(normed, qkv_weight[2], preferred_element_type=jnp.float32).astype(jnp.bfloat16)

    def split_heads(array):
        return array.reshape(tokens, heads, head_dim).transpose(1, 0, 2)

    def one_head(item):
        head_query, head_keys, head_values = item
        logits = jnp.dot(head_query, head_keys.T, preferred_element_type=jnp.float32) / math.sqrt(head_dim)
        probs = jnp.exp(logits - lax.optimization_barrier(jnp.max(logits, axis=-1, keepdims=True)))
        total = lax.optimization_barrier(jnp.sum(probs, axis=-1, keepdims=True))
        return (jnp.dot(probs.astype(jnp.bfloat16), head_values, preferred_element_type=jnp.float32) / total).astype(jnp.bfloat16)
    attended = lax.map(one_head, (split_heads(query), split_heads(keys), split_heads(values)))
    attended = attended.transpose(1, 0, 2).reshape(tokens, width)
    attn_sum = group_sum(attended, attn_out, N_VAR)
    updated = (stream.astype(jnp.float32) + attn_sum).astype(jnp.bfloat16)
    normed_two = layer_norm(updated, gain_two)
    hidden = jax.nn.gelu(jnp.dot(normed_two, mlp_in, preferred_element_type=jnp.float32), approximate=False).astype(jnp.bfloat16)
    mlp_sum = group_sum(hidden, mlp_out, N_VAR)
    return (updated.astype(jnp.float32) + mlp_sum).astype(jnp.bfloat16)
```

```python
import functools

import jax
import jax.numpy as jnp
from jax import lax
from jax.experimental import pallas as pl
from jax.experimental.pallas import tpu as pltpu
from jax.sharding import PartitionSpec as P

EPS = 1e-05
MESH = pl.DeviceIdType.MESH
BF = jnp.bfloat16
F32 = jnp.float32
GROUPS = 8
SHARE = 48
ROWS = 384
WIDTH = 1024
LANES = 128
LOCAL_VARS = 6
LOADS = 12


def mm(a, b):
    return jnp.dot(a, b, preferred_element_type=F32)


def mm_nt(a, b):
    return lax.dot_general(a, b, (((1,), (1,)), ((), ())), preferred_element_type=F32)


def lane_of(shape):
    return lax.broadcasted_iota(jnp.int32, shape, len(shape) - 1)


def split_three(value):
    high = value.astype(BF).astype(F32)
    rest = value - high
    middle = rest.astype(BF).astype(F32)
    return high, middle, rest - middle


def layer_norm(values, gain):
    center = values - jnp.mean(values, axis=-1, keepdims=True)
    spread = jnp.mean(center * center, axis=-1, keepdims=True)
    return (center * lax.rsqrt(spread + EPS) * gain).astype(BF)


def kernel(
    fields,
    var_embed,
    pos_embed,
    agg_key,
    agg_query,
    agg_value,
    agg_out,
    gain_one,
    qkv_weight,
    attn_out,
    gain_two,
    mlp_in,
    mlp_out,
    out,
    field_s,
    embed_s,
    pos_s,
    key_s,
    query_s,
    value_s,
    aggout_s,
    gain1_s,
    qkv_s,
    attnout_s,
    gain2_s,
    mlpin_s,
    mlpout_s,
    kq_s,
    spread_s,
    pick_s,
    emb_s,
    part_s,
    part_r,
    norm_r,
    q_s,
    qout_s,
    qin_r,
    kvout_s,
    kv_r,
    max_s,
    acc_s,
    att_s,
    att_r,
    upd_r,
    down_s,
    down_r,
    load_sem,
    field_sem,
    p1_send,
    p1_recv,
    p3_send,
    p3_recv,
    z_send,
    z_recv,
    kv_send,
    kv_recv,
    w_send,
    w_recv,
    a_send,
    a_recv,
    p8_send,
    p8_recv,
    p10_send,
    p10_recv,
):
    tok = lax.axis_index("tok")
    me = lax.axis_index("var")
    core = lax.rem(tok, 2)
    half = tok // 8
    ring = lax.rem(tok // 2, 4)
    sibling = tok + 1 - 2 * core
    partner = tok + 8 - 16 * half

    def along_x(step):
        return half * 8 + lax.rem(ring + step, 4) * 2 + core

    def peer(step):
        return lax.rem(me + 1 + step, GROUPS)

    def remote(src, dst, send, recv, to_tok, to_var):
        return pltpu.make_async_remote_copy(
            src_ref=src,
            dst_ref=dst,
            send_sem=send,
            recv_sem=recv,
            device_id=(to_tok, to_var),
            device_id_type=MESH,
        )

    barrier = pltpu.get_barrier_semaphore()
    others = [(tok, peer(i)) for i in range(GROUPS - 1)]
    others += [(partner, lax.rem(me + i, GROUPS)) for i in range(GROUPS)]
    others += [(sibling, me)] + [(along_x(i), me) for i in (1, 2, 3)]
    for device in others:
        pl.semaphore_signal(barrier, inc=1, device_id=device, device_id_type=MESH)

    def field_copy(i):
        rows = pl.ds(pl.multiple_of(peer(i) * SHARE, 16), SHARE)
        return pltpu.make_async_copy(fields.at[:, rows, :], field_s.at[i], field_sem.at[i])

    own_rows = pl.ds(pl.multiple_of(me * SHARE, 16), SHARE)
    loads = [
        pltpu.make_async_copy(src, dst, load_sem.at[k])
        for k, (src, dst) in enumerate(
            [
                (agg_query, query_s),
                (var_embed, embed_s),
                (agg_key, key_s),
                (agg_value, value_s),
                (agg_out, aggout_s),
                (pos_embed.at[own_rows, :], pos_s),
                (gain_one, gain1_s),
                (qkv_weight, qkv_s),
                (attn_out, attnout_s.at[me]),
                (gain_two, gain2_s),
                (mlp_in, mlpin_s),
                (mlp_out, mlpout_s),
            ]
        )
    ]
    for k in range(3):
        loads[k].start()
    field_copy(0).start()
    loads[3].start()
    for i in range(1, GROUPS):
        field_copy(i).start()
    for k in range(4, LOADS):
        loads[k].start()

    row = lax.broadcasted_iota(jnp.int32, (LANES, WIDTH), 0)
    col = lax.broadcasted_iota(jnp.int32, (LANES, WIDTH), 1)
    spread_s[...] = jnp.where((row < 32) & (row % 16 == col // 64), 1.0, 0.0).astype(BF)
    row = lax.broadcasted_iota(jnp.int32, (LANES, LANES), 0)
    col = lax.broadcasted_iota(jnp.int32, (LANES, LANES), 1)
    same = row % 16 == col % 16
    pick_s[0] = jnp.where(same & (row < 48), 1.0, 0.0).astype(BF)
    pick_s[1] = jnp.where(same & (row >= 48) & (row < 96), 1.0, 0.0).astype(BF)

    loads[0].wait()
    heads = query_s[...]
    tiled = jnp.concatenate([heads] * 16, axis=1)
    row = lax.broadcasted_iota(jnp.int32, (16, WIDTH), 0)
    col = lax.broadcasted_iota(jnp.int32, (16, WIDTH), 1)
    tiled = jnp.where(col // 64 == row, tiled, 0.0)
    stacked = jnp.concatenate(split_three(tiled), axis=0).astype(BF)
    loads[2].wait()
    folded = mm_nt(stacked, key_s[...])
    folded = ((folded[0:16] + folded[16:32] + folded[32:48]) * 0.125).astype(BF)
    kq_s[...] = jnp.concatenate([folded] * 8, axis=0)

    loads[1].wait()
    row = lax.broadcasted_iota(jnp.int32, (16, 48), 0)
    col = lax.broadcasted_iota(jnp.int32, (16, 48), 1)
    chosen = jnp.where((col == me * LOCAL_VARS + row) & (row < LOCAL_VARS), 1.0, 0.0).astype(BF)
    own_embed = mm(chosen, embed_s[...]).astype(BF)
    loads[3].wait()
    pl.semaphore_wait(barrier, len(others))

    lane = lane_of((SHARE, LANES))

    def aggregate_step(i, carry):
        field_copy(i).wait()
        for v in range(LOCAL_VARS):
            emb_s[v * SHARE : (v + 1) * SHARE, :] = field_s[i, v] + own_embed[v : v + 1, :]
        scores = mm_nt(emb_s[...], kq_s[...]).reshape(LOCAL_VARS, SHARE, LANES)
        highest = jnp.max(scores, axis=0)
        expd = jnp.exp(scores - highest[None])
        totals = jnp.sum(expd, axis=0)
        coarse = expd.astype(BF).astype(F32)
        weights = jnp.where((lane < 16)[None], coarse, jnp.where((lane < 32)[None], expd - coarse, 0.0))
        weights = weights.reshape(LOCAL_VARS * SHARE, LANES).astype(BF)
        for n in range(4):
            cols = slice(n * 256, (n + 1) * 256)
            wide = mm(weights, spread_s[:, cols])
            projected = mm(emb_s[...], value_s[:, cols])
            term = (wide * projected).reshape(LOCAL_VARS, SHARE, 256)
            part_s[i, :, cols] = jnp.sum(term, axis=0).astype(BF)
        high, middle, low = split_three(highest)
        high_t, middle_t, low_t = split_three(totals)
        notes = jnp.where(lane < 16, high, jnp.where(lane < 32, middle, low))
        notes_t = jnp.where(lane < 64, high_t, jnp.where(lane < 80, middle_t, low_t))
        part_s[i, :, WIDTH:] = jnp.where(lane < 48, notes, notes_t).astype(BF)

        @pl.when(i < GROUPS - 1)
        def _():
            remote(
                part_s.at[i], part_r.at[me], p1_send.at[i], p1_recv.at[me], tok, peer(i)
            ).start()

        return carry

    lax.fori_loop(0, GROUPS, aggregate_step, 0)
    part_r[me] = part_s[GROUPS - 1]

    def p1_copy(i):
        return remote(
            part_s.at[i], part_r.at[peer(i)], p1_send.at[i], p1_recv.at[peer(i)], tok, peer(i)
        )

    for i in range(GROUPS - 1):
        p1_copy(i).wait_recv()

    notes = part_r[:, :, WIDTH:].reshape(ROWS, LANES)
    highest = mm(notes, pick_s[0]).reshape(GROUPS, SHARE, LANES)
    totals = mm(notes, pick_s[1]).reshape(GROUPS, SHARE, LANES)
    scale = jnp.exp(highest - jnp.max(highest, axis=0)[None])
    scale = scale / jnp.sum(scale * totals, axis=0)[None]
    coarse = scale.astype(BF).astype(F32)
    scale = jnp.where((lane < 16)[None], coarse, jnp.where((lane < 32)[None], scale - coarse, 0.0))
    scale = scale.reshape(ROWS, LANES).astype(BF)
    mixed = []
    for n in range(4):
        cols = slice(n * 256, (n + 1) * 256)
        wide = mm(scale, spread_s[:, cols]).reshape(GROUPS, SHARE, 256)
        mixed.append(jnp.sum(wide * part_r[:, :, cols].astype(F32), axis=0).astype(BF))
    mixed = jnp.concatenate(mixed, axis=1)
    for k in (4, 5, 6):
        loads[k].wait()
    stream = (mm(mixed, aggout_s[...]) + pos_s[...].astype(F32)).astype(BF)
    norm_r[me] = layer_norm(stream.astype(F32), gain1_s[...])

    def gather_copy(buffer, send, recv, i, source):
        return remote(buffer.at[source], buffer.at[source], send.at[i], recv.at[source], tok, peer(i))

    for i in range(GROUPS - 1):
        gather_copy(norm_r, p3_send, p3_recv, i, me).start()
    loads[7].wait()
    loads[8].wait()
    for i in range(GROUPS - 1):
        gather_copy(norm_r, p3_send, p3_recv, i, peer(i)).wait_recv()

    normed = norm_r[...].reshape(ROWS, WIDTH)
    keys = mm(normed, qkv_s[1])
    values = mm(normed, qkv_s[2])
    wide_lane = lane_of((ROWS, LANES))
    left = wide_lane < 64
    kv_a = jnp.where(left, keys, pltpu.roll(values, 64, 1)).astype(BF)
    kv_b = jnp.where(left, pltpu.roll(keys, 64, 1), values).astype(BF)
    first = half == 0
    kv_r[core] = jnp.where(first, kv_a, kv_b)
    kvout_s[...] = jnp.where(first, kv_b, kv_a)

    def slot(order, owner):
        return order * 2 + owner

    z_kv = remote(kvout_s, kv_r.at[slot(1, core)], z_send.at[0], kv_recv.at[slot(1, core)], partner, me)
    z_kv.start()
    hops = ((2, 3), (3, 1), (4, 2))

    def x_copy(k, order, source):
        to = slot(order, core)
        return remote(
            kv_r.at[source], kv_r.at[to], kv_send.at[k], kv_recv.at[to], along_x(hops[k % 3][1]), me
        )

    for k in range(3):
        x_copy(k, hops[k][0], slot(0, core)).start()

    def share_copy(order, owner):
        at = slot(order, owner)
        return remote(kv_r.at[at], kv_r.at[at], kv_send.at[8 + order], kv_recv.at[at], sibling, me)

    share_copy(0, core).start()
    queries = mm(normed, qkv_s[0]) * 0.125
    rolled = pltpu.roll(queries, 64, 1)
    q_a = jnp.where(left, queries, 0.0).astype(BF)
    q_b = jnp.where(left, rolled, 0.0).astype(BF)
    q_s[0:ROWS, :] = jnp.where(first, q_a, q_b)
    other = jnp.where(first, rolled, queries)
    qout_s[...] = jnp.where(
        left[: ROWS // 2], other[: ROWS // 2], pltpu.roll(other[ROWS // 2 :], 64, 1)
    ).astype(BF)
    z_q = remote(qout_s, qin_r, z_send.at[1], z_recv.at[0], partner, me)
    z_q.start()

    w_rows = pl.ds(pl.multiple_of(core * 64, 64), 64)

    def w_copy(i, source):
        at = attnout_s.at[source, w_rows, :]
        return remote(at, at, w_send.at[i], w_recv.at[source], tok, peer(i))

    for i in range(GROUPS - 1):
        w_copy(i, me).start()

    max_s[...] = jnp.full(max_s.shape, -jnp.inf, F32)
    acc_s[...] = jnp.zeros(acc_s.shape, F32)
    z_kv.wait_recv()
    for k in range(3):
        x_copy(3 + k, hops[k][0] + 3, slot(1, core)).start()
    z_q.wait_recv()
    packed = qin_r[...].astype(F32)
    q_s[ROWS : ROWS + ROWS // 2, :] = jnp.where(left[: ROWS // 2], packed, 0.0).astype(BF)
    q_s[ROWS + ROWS // 2 :, :] = jnp.where(
        left[: ROWS // 2], pltpu.roll(packed, 64, 1), 0.0
    ).astype(BF)

    def absorb(at):
        block = kv_r[at]
        ones = jnp.where(left, 1.0, block.astype(F32)).astype(BF)
        for n in range(3):
            rows = slice(n * 256, (n + 1) * 256)
            logits = mm_nt(q_s[rows, :], block)
            before = max_s[rows, :]
            newest = jnp.maximum(before, jnp.max(logits, axis=1, keepdims=True))
            probs = jnp.exp(logits - jnp.concatenate([newest] * 3, axis=1)).astype(BF)
            acc_s[rows, :] = acc_s[rows, :] * jnp.exp(before - newest) + mm(probs, ones)
            max_s[rows, :] = newest

    def attend_step(order, carry):
        own = slot(order, core)
        theirs = slot(order, 1 - core)

        @pl.when(order > 1)
        def _():
            remote(kv_r.at[own], kv_r.at[own], kv_send.at[0], kv_recv.at[own], sibling, me).wait_recv()

        @pl.when(order > 0)
        def _():
            share_copy(order, core).start()

        absorb(own)
        share_copy(order, 1 - core).wait_recv()
        absorb(theirs)
        return carry

    lax.fori_loop(0, 8, attend_step, 0)

    acc = acc_s[...]
    turned = pltpu.roll(acc, 64, 1)
    wide_left = lane_of((2 * ROWS, LANES)) < 64
    result = jnp.where(wide_left, turned, acc) / jnp.where(wide_left, acc, turned)
    keep = wide_left == jnp.broadcast_to(first, wide_left.shape)
    att_s[...] = jnp.where(keep, result, 0.0).astype(BF).reshape(2, GROUPS, SHARE, LANES)
    att_r[half, me] = att_s[0, me]

    def att_copy(side, i, at, source):
        to = lax.rem(me + 1 + i, GROUPS)
        return remote(
            att_s.at[side, to],
            att_r.at[at, source],
            a_send.at[side * GROUPS + i],
            a_recv.at[at * GROUPS + source],
            tok if side == 0 else partner,
            to,
        )

    for i in range(GROUPS - 1):
        att_copy(0, i, half, me).start()
        att_copy(1, i, half, me).start()
    att_copy(1, GROUPS - 1, half, me).start()

    def w_share(i, rows):
        at = attnout_s.at[peer(i), rows, :]
        return remote(at, at, w_send.at[GROUPS + i], w_recv.at[GROUPS + peer(i)], sibling, me)

    their_rows = pl.ds(pl.multiple_of(64 - core * 64, 64), 64)
    for i in range(GROUPS - 1):
        w_copy(i, peer(i)).wait_recv()
        w_share(i, w_rows).start()
    for i in range(GROUPS - 1):
        w_share(i, their_rows).wait_recv()
    for i in range(GROUPS - 1):
        att_copy(0, i, half, peer(i)).wait_recv()
    for i in range(GROUPS):
        att_copy(1, i, 1 - half, peer(i)).wait_recv()

    attended = jnp.concatenate([att_r[0, g] + att_r[1, g] for g in range(GROUPS)], axis=1)
    attn_sum = mm(attended, attnout_s[...].reshape(WIDTH, WIDTH))
    upd_r[me] = (stream.astype(F32) + attn_sum).astype(BF)
    for i in range(GROUPS - 1):
        gather_copy(upd_r, p8_send, p8_recv, i, me).start()
    for k in (9, 10, 11):
        loads[k].wait()
    for i in range(GROUPS - 1):
        gather_copy(upd_r, p8_send, p8_recv, i, peer(i)).wait_recv()

    updated = upd_r[...].reshape(ROWS, WIDTH)
    normed_two = layer_norm(updated.astype(F32), gain2_s[...])
    raised = mm(normed_two, mlpin_s[...])
    hidden = (0.5 * raised * (1.0 + lax.erf(raised * 0.7071067811865476))).astype(BF)
    for n in range(4):
        terms = mm(hidden, mlpout_s[:, n * 256 : (n + 1) * 256]).astype(BF)
        down_s[2 * n] = terms[:, :LANES]
        down_s[2 * n + 1] = terms[:, LANES:]

    def down_copy(i, source):
        return remote(
            down_s.at[peer(i)],
            down_r.at[source],
            p10_send.at[i],
            p10_recv.at[source],
            tok,
            peer(i),
        )

    for i in range(GROUPS - 1):
        down_copy(i, me).start()
    total = down_s[me].astype(F32)
    own_cols = pl.ds(pl.multiple_of(me * LANES, LANES), LANES)
    residual = upd_r[:, :, own_cols].reshape(ROWS, LANES).astype(F32)
    for i in range(GROUPS - 1):
        down_copy(i, peer(i)).wait_recv()
        total = total + down_r[peer(i)].astype(F32)
    out[...] = (residual + total).astype(BF)

    for i in range(GROUPS - 1):
        p1_copy(i).wait_send()
        gather_copy(norm_r, p3_send, p3_recv, i, me).wait_send()
        w_copy(i, me).wait_send()
        w_share(i, w_rows).wait_send()
        att_copy(0, i, half, me).wait_send()
        gather_copy(upd_r, p8_send, p8_recv, i, me).wait_send()
        down_copy(i, me).wait_send()
    for i in range(GROUPS):
        att_copy(1, i, half, me).wait_send()
        share_copy(i, core).wait_send()
    for k in range(3):
        x_copy(k, hops[k][0], slot(0, core)).wait_send()
        x_copy(3 + k, hops[k][0] + 3, slot(1, core)).wait_send()
    z_kv.wait_send()
    z_q.wait_send()


def scratch():
    vmem = pltpu.VMEM
    dma = pltpu.SemaphoreType.DMA
    return [
        vmem((GROUPS, LOCAL_VARS, SHARE, WIDTH), BF),
        vmem((48, WIDTH), BF),
        vmem((SHARE, WIDTH), BF),
        vmem((WIDTH, WIDTH), BF),
        vmem((16, 64), F32),
        vmem((WIDTH, WIDTH), BF),
        vmem((WIDTH, WIDTH), BF),
        vmem((1, WIDTH), F32),
        vmem((3, WIDTH, LANES), BF),
        vmem((GROUPS, LANES, WIDTH), BF),
        vmem((1, WIDTH), F32),
        vmem((WIDTH, 512), BF),
        vmem((512, WIDTH), BF),
        vmem((LANES, WIDTH), BF),
        vmem((LANES, WIDTH), BF),
        vmem((2, LANES, LANES), BF),
        vmem((LOCAL_VARS * SHARE, WIDTH), BF),
        vmem((GROUPS, SHARE, WIDTH + LANES), BF),
        vmem((GROUPS, SHARE, WIDTH + LANES), BF),
        vmem((GROUPS, SHARE, WIDTH), BF),
        vmem((2 * ROWS, LANES), BF),
        vmem((ROWS // 2, LANES), BF),
        vmem((ROWS // 2, LANES), BF),
        vmem((ROWS, LANES), BF),
        vmem((16, ROWS, LANES), BF),
        vmem((2 * ROWS, LANES), F32),
        vmem((2 * ROWS, LANES), F32),
        vmem((2, GROUPS, SHARE, LANES), BF),
        vmem((2, GROUPS, SHARE, LANES), BF),
        vmem((GROUPS, SHARE, WIDTH), BF),
        vmem((GROUPS, ROWS, LANES), BF),
        vmem((GROUPS, ROWS, LANES), BF),
        dma((LOADS,)),
        dma((GROUPS,)),
        dma((GROUPS,)),
        dma((GROUPS,)),
        dma((GROUPS,)),
        dma((GROUPS,)),
        dma((2,)),
        dma((1,)),
        dma((16,)),
        dma((16,)),
        dma((2 * GROUPS,)),
        dma((2 * GROUPS,)),
        dma((2 * GROUPS,)),
        dma((2 * GROUPS,)),
        dma((GROUPS,)),
        dma((GROUPS,)),
        dma((GROUPS,)),
        dma((GROUPS,)),
    ]


def body(
    fields,
    var_embed,
    pos_embed,
    agg_key,
    agg_query,
    agg_value,
    agg_out,
    gain_one,
    qkv_weight,
    attn_out,
    gain_two,
    mlp_in,
    mlp_out,
):
    return pl.pallas_call(
        kernel,
        out_shape=jax.ShapeDtypeStruct((ROWS, LANES), BF),
        in_specs=[pl.BlockSpec(memory_space=pl.ANY)] * 13,
        out_specs=pl.BlockSpec(memory_space=pltpu.VMEM),
        scratch_shapes=scratch(),
        compiler_params=pltpu.CompilerParams(
            collective_id=0, has_side_effects=True, vmem_limit_bytes=56 * 2**20
        ),
    )(
        fields,
        var_embed,
        pos_embed,
        agg_key,
        agg_query,
        agg_value,
        agg_out,
        gain_one.reshape(1, WIDTH),
        qkv_weight,
        attn_out,
        gain_two.reshape(1, WIDTH),
        mlp_in,
        mlp_out,
    )


def solution(mesh):
    placed = (
        P("var", "tok", None),
        P(),
        P("tok", None),
        P(),
        P(),
        P(),
        P(),
        P(),
        P(None, None, "var"),
        P("var", None),
        P(),
        P(None, "var"),
        P("var", None),
    )
    return jax.shard_map(
        body, mesh=mesh, in_specs=placed, out_specs=P("tok", "var"), check_vma=False
    )
```

```python
import functools

import jax
import jax.numpy as jnp
from jax import lax
from jax.experimental import pallas as pl
from jax.experimental.pallas import tpu as pltpu
from jax.sharding import PartitionSpec as P

EPS = 1e-05
MESH = pl.DeviceIdType.MESH
BF = jnp.bfloat16
F32 = jnp.float32
GROUPS = 8
SHARE = 48
ROWS = 384
WIDTH = 1024
LANES = 128
LOCAL_VARS = 6
LOADS = 12


def mm(a, b):
    return jnp.dot(a, b, preferred_element_type=F32)


def mm_nt(a, b):
    return lax.dot_general(a, b, (((1,), (1,)), ((), ())), preferred_element_type=F32)


def lane_of(shape):
    return lax.broadcasted_iota(jnp.int32, shape, len(shape) - 1)


def split_three(value):
    high = value.astype(BF).astype(F32)
    rest = value - high
    middle = rest.astype(BF).astype(F32)
    return high, middle, rest - middle


def layer_norm(values, gain):
    center = values - jnp.mean(values, axis=-1, keepdims=True)
    spread = jnp.mean(center * center, axis=-1, keepdims=True)
    return (center * lax.rsqrt(spread + EPS) * gain).astype(BF)


def kernel(
    fields,
    var_embed,
    pos_embed,
    agg_key,
    agg_query,
    agg_value,
    agg_out,
    gain_one,
    qkv_weight,
    attn_out,
    gain_two,
    mlp_in,
    mlp_out,
    out,
    field_s,
    embed_s,
    pos_s,
    key_s,
    query_s,
    value_s,
    aggout_s,
    gain1_s,
    qkv_s,
    attnout_s,
    gain2_s,
    mlpin_s,
    mlpout_s,
    kq_s,
    spread_s,
    pick_s,
    emb_s,
    weight_s,
    part_s,
    part_r,
    norm_r,
    q_s,
    qout_s,
    qin_r,
    kvout_s,
    kv_r,
    max_s,
    acc_s,
    att_s,
    att_r,
    upd_r,
    res_r,
    down_s,
    down_r,
    load_sem,
    field_sem,
    p1_send,
    p1_recv,
    p3_send,
    p3_recv,
    z_send,
    z_recv,
    kv_send,
    kv_recv,
    w_send,
    w_recv,
    v_send,
    v_recv,
    a_send,
    a_recv,
    p8_send,
    p8_recv,
    p10_send,
    p10_recv,
):
    tok = lax.axis_index("tok")
    me = lax.axis_index("var")
    core = lax.rem(tok, 2)
    half = tok // 8
    ring = lax.rem(tok // 2, 4)
    sibling = tok + 1 - 2 * core
    partner = tok + 8 - 16 * half

    def along_x(step):
        return half * 8 + lax.rem(ring + step, 4) * 2 + core

    plane = me // 4
    high_y = lax.rem(me, 4)

    def peer(step):
        return lax.rem(plane + 1 + step // 4, 2) * 4 + lax.rem(high_y + 3 - step % 4, 4)

    def remote(src, dst, send, recv, to_tok, to_var):
        return pltpu.make_async_remote_copy(
            src_ref=src,
            dst_ref=dst,
            send_sem=send,
            recv_sem=recv,
            device_id=(to_tok, to_var),
            device_id_type=MESH,
        )

    barrier = pltpu.get_barrier_semaphore()
    others = [(tok, peer(i)) for i in range(GROUPS - 1)]
    others += [(partner, lax.rem(me + i, GROUPS)) for i in range(GROUPS)]
    others += [(sibling, me)] + [(along_x(i), me) for i in (1, 2, 3)]
    for device in others:
        pl.semaphore_signal(barrier, inc=1, device_id=device, device_id_type=MESH)

    def field_copy(i):
        rows = pl.ds(pl.multiple_of(peer(i) * SHARE, 16), SHARE)
        return pltpu.make_async_copy(fields.at[:, rows, :], field_s.at[i], field_sem.at[i])

    own_rows = pl.ds(pl.multiple_of(me * SHARE, 16), SHARE)
    loads = [
        pltpu.make_async_copy(src, dst, load_sem.at[k])
        for k, (src, dst) in enumerate(
            [
                (agg_query, query_s),
                (var_embed, embed_s),
                (agg_key, key_s),
                (agg_value, value_s),
                (agg_out, aggout_s),
                (pos_embed.at[own_rows, :], pos_s),
                (gain_one, gain1_s),
                (qkv_weight, qkv_s),
                (attn_out.at[ring, core], attnout_s.at[me, ring, core]),
                (gain_two, gain2_s),
                (mlp_in, mlpin_s.at[0]),
                (mlp_out, mlpout_s.at[0]),
            ]
        )
    ]
    for k in (8, 0, 1, 2):
        loads[k].start()
    field_copy(0).start()
    loads[3].start()
    field_copy(1).start()

    row = lax.broadcasted_iota(jnp.int32, (LANES, WIDTH), 0)
    col = lax.broadcasted_iota(jnp.int32, (LANES, WIDTH), 1)
    spread_s[...] = jnp.where((row < 32) & (row % 16 == col // 64), 1.0, 0.0).astype(BF)
    row = lax.broadcasted_iota(jnp.int32, (LANES, LANES), 0)
    col = lax.broadcasted_iota(jnp.int32, (LANES, LANES), 1)
    same = row % 16 == col % 16
    pick_s[0] = jnp.where(same & (row < 48), 1.0, 0.0).astype(BF)
    pick_s[1] = jnp.where(same & (row >= 48) & (row < 96), 1.0, 0.0).astype(BF)

    loads[0].wait()
    heads = query_s[...]
    tiled = jnp.concatenate([heads] * 16, axis=1)
    row = lax.broadcasted_iota(jnp.int32, (16, WIDTH), 0)
    col = lax.broadcasted_iota(jnp.int32, (16, WIDTH), 1)
    tiled = jnp.where(col // 64 == row, tiled, 0.0)
    stacked = jnp.concatenate(split_three(tiled) + (jnp.zeros((80, WIDTH), F32),), axis=0)
    stacked = stacked.T.astype(BF)
    loads[2].wait()
    folded = mm(key_s[...], stacked)
    folded = folded + pltpu.roll(folded, 112, 1) + pltpu.roll(folded, 96, 1)
    folded = jnp.where(lane_of((WIDTH, LANES)) < 16, folded * 0.125, 0.0)
    for shift in (16, 32, 64):
        folded = folded + pltpu.roll(folded, shift, 1)
    kq_s[...] = folded.astype(BF)

    loads[1].wait()
    row = lax.broadcasted_iota(jnp.int32, (16, 48), 0)
    col = lax.broadcasted_iota(jnp.int32, (16, 48), 1)
    chosen = jnp.where((col == me * LOCAL_VARS + row) & (row < LOCAL_VARS), 1.0, 0.0).astype(BF)
    own_embed = mm(chosen, embed_s[...]).astype(BF)

    across = lax.rem(me + 4, GROUPS)
    mlp = (mlpin_s, mlpout_s)

    def w_copy(i, source):
        at = attnout_s.at[source, ring, core]
        return remote(at, at, w_send.at[i], w_recv.at[source], tok, peer(i))

    def mlp_copy(k):
        return remote(
            mlp[k].at[0, ring, core], mlp[k].at[1, ring, core], w_send.at[8 + k], w_recv.at[8 + k], tok, across
        )

    def spread_copy(k, step, place):
        at = attnout_s.at[:, place, core] if k == 2 else mlp[k].at[1, place, core]
        n = k * 3 + step - 1
        return remote(at, at, v_send.at[n], v_recv.at[n], along_x(step), me)

    def pair_copy(k, owner):
        at = attnout_s.at[:, :, owner] if k == 2 else mlp[k].at[1, :, owner]
        return remote(at, at, v_send.at[9 + k], v_recv.at[9 + k], sibling, me)

    def spread_arrived(k):
        for step in (1, 2, 3):
            spread_copy(k, step, lax.rem(ring + 4 - step, 4)).wait_recv()

    lane = lane_of((SHARE, LANES))

    def p1_copy(i, source):
        return remote(
            part_s.at[i], part_r.at[source], p1_send.at[i], p1_recv.at[source], tok, peer(i)
        )

    def weigh(i):
        at = i % 2
        for v in range(LOCAL_VARS):
            emb_s[at, v * SHARE : (v + 1) * SHARE, :] = field_s[i, v] + own_embed[v : v + 1, :]
        scores = mm(emb_s[at], kq_s[...]).reshape(LOCAL_VARS, SHARE, LANES)
        highest = jnp.max(scores, axis=0)
        expd = jnp.exp(scores - highest[None])
        totals = jnp.sum(expd, axis=0)
        coarse = expd.astype(BF).astype(F32)
        weights = jnp.where((lane < 16)[None], coarse, jnp.where((lane < 32)[None], expd - coarse, 0.0))
        weight_s[at] = weights.reshape(LOCAL_VARS * SHARE, LANES).astype(BF)
        high, middle, low = split_three(highest)
        high_t, middle_t, low_t = split_three(totals)
        notes = jnp.where(lane < 16, high, jnp.where(lane < 32, middle, low))
        notes_t = jnp.where(lane < 64, high_t, jnp.where(lane < 80, middle_t, low_t))
        part_s[i, :, WIDTH:] = jnp.where(lane < 48, notes, notes_t).astype(BF)

    def add_up(i):
        at = i % 2
        for n in range(2):
            cols = slice(n * 512, (n + 1) * 512)
            wide = mm(weight_s[at], spread_s[:, cols])
            projected = mm(emb_s[at], value_s[:, cols])
            term = (wide * projected).reshape(LOCAL_VARS, SHARE, 512)
            part_s[i, :, cols] = jnp.sum(term, axis=0).astype(BF)

    field_copy(0).wait()
    weigh(0)
    loads[3].wait()
    for i in range(GROUPS):
        if i + 2 < GROUPS:
            field_copy(i + 2).start()
        if i == 1:
            for k in (4, 5, 6, 7):
                loads[k].start()
        if i == 4:
            for k in (9, 10, 11):
                loads[k].start()
        if i + 1 < GROUPS:
            field_copy(i + 1).wait()
            weigh(i + 1)
        add_up(i)
        if i == 2:
            pl.semaphore_wait(barrier, len(others))
            for k in range(3):
                p1_copy(k, me).start()
        elif 2 < i < GROUPS - 1:
            p1_copy(i, me).start()
    loads[8].wait()
    for i in range(GROUPS - 1):
        w_copy(i, me).start()
    part_r[me] = part_s[GROUPS - 1]
    for i in range(GROUPS - 1):
        p1_copy(i, peer(i)).wait_recv()

    notes = part_r[:, :, WIDTH:].reshape(ROWS, LANES)
    highest = mm(notes, pick_s[0]).reshape(GROUPS, SHARE, LANES)
    totals = mm(notes, pick_s[1]).reshape(GROUPS, SHARE, LANES)
    scale = jnp.exp(highest - jnp.max(highest, axis=0)[None])
    scale = scale / jnp.sum(scale * totals, axis=0)[None]
    coarse = scale.astype(BF).astype(F32)
    scale = jnp.where((lane < 16)[None], coarse, jnp.where((lane < 32)[None], scale - coarse, 0.0))
    scale = scale.reshape(ROWS, LANES).astype(BF)
    mixed = []
    for n in range(4):
        cols = slice(n * 256, (n + 1) * 256)
        wide = mm(scale, spread_s[:, cols]).reshape(GROUPS, SHARE, 256)
        mixed.append(jnp.sum(wide * part_r[:, :, cols].astype(F32), axis=0).astype(BF))
    mixed = jnp.concatenate(mixed, axis=1)
    for k in (4, 5, 6):
        loads[k].wait()
    stream = (mm(mixed, aggout_s[...]) + pos_s[...].astype(F32)).astype(BF)
    norm_r[me] = layer_norm(stream.astype(F32), gain1_s[...])

    def gather_copy(buffer, send, recv, i, source):
        return remote(buffer.at[source], buffer.at[source], send.at[i], recv.at[source], tok, peer(i))

    for i in range(GROUPS - 1):
        gather_copy(norm_r, p3_send, p3_recv, i, me).start()
    loads[7].wait()
    for i in range(GROUPS - 1):
        w_copy(i, peer(i)).wait_recv()
    for step in (1, 2, 3):
        spread_copy(2, step, ring).start()
    for i in range(GROUPS - 1):
        gather_copy(norm_r, p3_send, p3_recv, i, peer(i)).wait_recv()

    normed = norm_r[...].reshape(ROWS, WIDTH)
    keys = mm(normed, qkv_s[1])
    values = mm(normed, qkv_s[2])
    wide_lane = lane_of((ROWS, LANES))
    left = wide_lane < 64
    kv_a = jnp.where(left, keys, pltpu.roll(values, 64, 1)).astype(BF)
    kv_b = jnp.where(left, pltpu.roll(keys, 64, 1), values).astype(BF)
    first = half == 0
    kv_r[core] = jnp.where(first, kv_a, kv_b)
    kvout_s[...] = jnp.where(first, kv_b, kv_a)

    def slot(order, owner):
        return order * 2 + owner

    z_kv = remote(kvout_s, kv_r.at[slot(1, core)], z_send.at[0], kv_recv.at[slot(1, core)], partner, me)
    z_kv.start()
    hops = ((2, 3), (3, 1), (4, 2))

    def x_copy(k, order, source):
        to = slot(order, core)
        return remote(
            kv_r.at[source], kv_r.at[to], kv_send.at[k], kv_recv.at[to], along_x(hops[k % 3][1]), me
        )

    for k in range(3):
        x_copy(k, hops[k][0], slot(0, core)).start()

    def share_copy(order, owner):
        at = slot(order, owner)
        return remote(kv_r.at[at], kv_r.at[at], kv_send.at[8 + order], kv_recv.at[at], sibling, me)

    share_copy(0, core).start()
    queries = mm(normed, qkv_s[0]) * 0.125
    rolled = pltpu.roll(queries, 64, 1)
    q_a = jnp.where(left, queries, 0.0).astype(BF)
    q_b = jnp.where(left, rolled, 0.0).astype(BF)
    q_s[0:ROWS, :] = jnp.where(first, q_a, q_b)
    other = jnp.where(first, rolled, queries)
    qout_s[...] = jnp.where(
        left[: ROWS // 2], other[: ROWS // 2], pltpu.roll(other[ROWS // 2 :], 64, 1)
    ).astype(BF)
    z_q = remote(qout_s, qin_r, z_send.at[1], z_recv.at[0], partner, me)
    z_q.start()
    for k in (10, 11):
        loads[k].wait()
    for k in range(2):
        mlp_copy(k).start()

    spread_arrived(2)
    pair_copy(2, core).start()
    max_s[...] = jnp.full(max_s.shape, -jnp.inf, F32)
    acc_s[...] = jnp.zeros(acc_s.shape, F32)
    z_kv.wait_recv()
    for k in range(3):
        x_copy(3 + k, hops[k][0] + 3, slot(1, core)).start()
    z_q.wait_recv()
    packed = qin_r[...].astype(F32)
    q_s[ROWS : ROWS + ROWS // 2, :] = jnp.where(left[: ROWS // 2], packed, 0.0).astype(BF)
    q_s[ROWS + ROWS // 2 :, :] = jnp.where(
        left[: ROWS // 2], pltpu.roll(packed, 64, 1), 0.0
    ).astype(BF)

    def pass_on(order):
        share_copy(order, core).wait_recv()
        share_copy(order, core).start()

    share_copy(1, core).start()
    pass_on(2)
    pass_on(3)
    many_left = lane_of((4 * ROWS, LANES)) < 64

    def attend_step(step, carry):
        @pl.when(step == 1)
        def _():
            pass_on(4)

        @pl.when(step == 2)
        def _():
            pass_on(5)
            pass_on(6)

        @pl.when(step == 3)
        def _():
            pass_on(7)
            for k in range(2):
                mlp_copy(k).wait_recv()
                for hop in (1, 2, 3):
                    spread_copy(k, hop, ring).start()

        for order in (2 * step, 2 * step + 1):
            share_copy(order, 1 - core).wait_recv()
        block = kv_r[pl.ds(step * 4, 4)].reshape(4 * ROWS, LANES)
        ones = jnp.where(many_left, 1.0, block.astype(F32)).astype(BF)
        logits = mm_nt(q_s[...], block)
        before = max_s[...]
        newest = jnp.maximum(before, jnp.max(logits, axis=1, keepdims=True))
        probs = jnp.exp(logits - jnp.concatenate([newest] * 12, axis=1)).astype(BF)
        acc_s[...] = acc_s[...] * jnp.exp(before - newest) + mm(probs, ones)
        max_s[...] = newest
        return carry

    lax.fori_loop(0, 4, attend_step, 0)

    acc = acc_s[...]
    turned = pltpu.roll(acc, 64, 1)
    wide_left = lane_of((2 * ROWS, LANES)) < 64
    result = jnp.where(wide_left, turned, acc) / jnp.where(wide_left, acc, turned)
    keep = wide_left == jnp.broadcast_to(first, wide_left.shape)
    att_s[...] = jnp.where(keep, result, 0.0).astype(BF).reshape(2, GROUPS, SHARE, LANES)
    att_r[half, me] = att_s[0, me]

    def att_copy(side, i, at, source):
        to = peer(i)
        return remote(
            att_s.at[side, to],
            att_r.at[at, source],
            a_send.at[side * GROUPS + i],
            a_recv.at[at * GROUPS + source],
            tok if side == 0 else partner,
            to,
        )

    for i in range(GROUPS - 1):
        att_copy(0, i, half, me).start()
        att_copy(1, i, half, me).start()
    att_copy(1, GROUPS - 1, half, me).start()

    for i in range(GROUPS - 1):
        att_copy(0, i, half, peer(i)).wait_recv()
    for i in range(GROUPS):
        att_copy(1, i, 1 - half, peer(i)).wait_recv()

    pair_copy(2, 1 - core).wait_recv()
    attended = jnp.concatenate([att_r[0, g] + att_r[1, g] for g in range(GROUPS)], axis=1)
    attn_sum = mm(attended, attnout_s[...].reshape(WIDTH, WIDTH))
    def along_y(i):
        return lax.rem(high_y + 1 + i, 4)

    def upd_copy(i, source):
        at = upd_r.at[source]
        return remote(at, at, p8_send.at[i], p8_recv.at[source], tok, plane * 4 + along_y(i))

    def res_copy(i, source):
        to = (1 - plane) * 4 + i
        cols = pl.ds(pl.multiple_of(to * LANES, LANES), LANES)
        return remote(
            upd_r.at[high_y, :, cols], res_r.at[source], p8_send.at[4 + i], p8_recv.at[4 + source], tok, to
        )

    upd_r[high_y] = (stream.astype(F32) + attn_sum).astype(BF)
    for i in range(3):
        upd_copy(i, high_y).start()
    for i in range(4):
        res_copy(i, high_y).start()
    loads[9].wait()
    for k in range(2):
        spread_arrived(k)
        pair_copy(k, core).start()
    for i in range(3):
        upd_copy(i, along_y(i)).wait_recv()

    updated = upd_r[...].reshape(ROWS // 2, WIDTH)
    normed_two = layer_norm(updated.astype(F32), gain2_s[...])
    for k in range(2):
        pair_copy(k, 1 - core).wait_recv()
    hidden = []
    for k in range(2):
        raised = mm(normed_two, mlpin_s[k].reshape(WIDTH, 512))
        hidden.append((0.5 * raised * (1.0 + lax.erf(raised * 0.7071067811865476))).astype(BF))
    hidden = jnp.concatenate(hidden, axis=1)
    down_weight = mlpout_s[...].reshape(WIDTH, WIDTH)
    for n in range(4):
        terms = mm(hidden, down_weight[:, n * 256 : (n + 1) * 256]).astype(BF)
        down_s[2 * n] = terms[:, :LANES]
        down_s[2 * n + 1] = terms[:, LANES:]

    def down_copy(i, source):
        return remote(
            down_s.at[peer(i)],
            down_r.at[source],
            p10_send.at[i],
            p10_recv.at[source],
            tok,
            peer(i),
        )

    for i in range(GROUPS - 1):
        down_copy(i, me).start()
    down_r[me] = down_s[me]
    own_cols = pl.ds(pl.multiple_of(me * LANES, LANES), LANES)
    for i in range(4):
        res_copy(i, i).wait_recv()
    for i in range(GROUPS - 1):
        down_copy(i, peer(i)).wait_recv()

    def finish_half(which, residual):
        terms = jnp.sum(down_r[pl.ds(which * 4, 4)].astype(F32), axis=0)
        rows = pl.ds(pl.multiple_of(which * (ROWS // 2), 16), ROWS // 2)
        out[rows, :] = (residual.reshape(ROWS // 2, LANES).astype(F32) + terms).astype(BF)

    finish_half(plane, upd_r[:, :, own_cols])
    finish_half(1 - plane, res_r[...])

    for i in range(GROUPS - 1):
        p1_copy(i, me).wait_send()
        gather_copy(norm_r, p3_send, p3_recv, i, me).wait_send()
        w_copy(i, me).wait_send()
        att_copy(0, i, half, me).wait_send()
        down_copy(i, me).wait_send()
    for i in range(GROUPS):
        att_copy(1, i, half, me).wait_send()
        share_copy(i, core).wait_send()
    for k in range(3):
        x_copy(k, hops[k][0], slot(0, core)).wait_send()
        x_copy(3 + k, hops[k][0] + 3, slot(1, core)).wait_send()
    z_kv.wait_send()
    z_q.wait_send()
    for i in range(3):
        upd_copy(i, high_y).wait_send()
        pair_copy(i, core).wait_send()
        for step in (1, 2, 3):
            spread_copy(i, step, ring).wait_send()
    for i in range(4):
        res_copy(i, high_y).wait_send()
    for k in range(2):
        mlp_copy(k).wait_send()


def scratch():
    vmem = pltpu.VMEM
    dma = pltpu.SemaphoreType.DMA
    return [
        vmem((GROUPS, LOCAL_VARS, SHARE, WIDTH), BF),
        vmem((48, WIDTH), BF),
        vmem((SHARE, WIDTH), BF),
        vmem((WIDTH, WIDTH), BF),
        vmem((16, 64), F32),
        vmem((WIDTH, WIDTH), BF),
        vmem((WIDTH, WIDTH), BF),
        vmem((1, WIDTH), F32),
        vmem((3, WIDTH, LANES), BF),
        vmem((GROUPS, 4, 2, 16, WIDTH), BF),
        vmem((1, WIDTH), F32),
        vmem((2, 4, 2, LANES, 512), BF),
        vmem((2, 4, 2, 64, WIDTH), BF),
        vmem((WIDTH, LANES), BF),
        vmem((LANES, WIDTH), BF),
        vmem((2, LANES, LANES), BF),
        vmem((2, LOCAL_VARS * SHARE, WIDTH), BF),
        vmem((2, LOCAL_VARS * SHARE, LANES), BF),
        vmem((GROUPS, SHARE, WIDTH + LANES), BF),
        vmem((GROUPS, SHARE, WIDTH + LANES), BF),
        vmem((GROUPS, SHARE, WIDTH), BF),
        vmem((2 * ROWS, LANES), BF),
        vmem((ROWS // 2, LANES), BF),
        vmem((ROWS // 2, LANES), BF),
        vmem((ROWS, LANES), BF),
        vmem((16, ROWS, LANES), BF),
        vmem((2 * ROWS, LANES), F32),
        vmem((2 * ROWS, LANES), F32),
        vmem((2, GROUPS, SHARE, LANES), BF),
        vmem((2, GROUPS, SHARE, LANES), BF),
        vmem((4, SHARE, WIDTH), BF),
        vmem((4, SHARE, LANES), BF),
        vmem((GROUPS, ROWS // 2, LANES), BF),
        vmem((GROUPS, ROWS // 2, LANES), BF),
        dma((LOADS,)),
        dma((GROUPS,)),
        dma((GROUPS,)),
        dma((GROUPS,)),
        dma((GROUPS,)),
        dma((GROUPS,)),
        dma((2,)),
        dma((1,)),
        dma((16,)),
        dma((16,)),
        dma((12,)),
        dma((12,)),
        dma((2 * GROUPS,)),
        dma((2 * GROUPS,)),
        dma((2 * GROUPS,)),
        dma((2 * GROUPS,)),
        dma((GROUPS,)),
        dma((GROUPS,)),
        dma((GROUPS,)),
        dma((GROUPS,)),
    ]


def body(
    fields,
    var_embed,
    pos_embed,
    agg_key,
    agg_query,
    agg_value,
    agg_out,
    gain_one,
    qkv_weight,
    attn_out,
    gain_two,
    mlp_in,
    mlp_out,
):
    return pl.pallas_call(
        kernel,
        out_shape=jax.ShapeDtypeStruct((ROWS, LANES), BF),
        in_specs=[pl.BlockSpec(memory_space=pl.ANY)] * 13,
        out_specs=pl.BlockSpec(memory_space=pltpu.VMEM),
        scratch_shapes=scratch(),
        compiler_params=pltpu.CompilerParams(
            collective_id=0, has_side_effects=True, vmem_limit_bytes=56 * 2**20
        ),
    )(
        fields,
        var_embed,
        pos_embed,
        agg_key,
        agg_query,
        agg_value,
        agg_out,
        gain_one.reshape(1, WIDTH),
        qkv_weight,
        attn_out.reshape(4, 2, 16, WIDTH),
        gain_two.reshape(1, WIDTH),
        mlp_in.reshape(4, 2, LANES, 512),
        mlp_out.reshape(4, 2, 64, WIDTH),
    )


def solution(mesh):
    placed = (
        P("var", "tok", None),
        P(),
        P("tok", None),
        P(),
        P(),
        P(),
        P(),
        P(),
        P(None, None, "var"),
        P("var", None),
        P(),
        P(None, "var"),
        P("var", None),
    )
    return jax.shard_map(
        body, mesh=mesh, in_specs=placed, out_specs=P("tok", "var"), check_vma=False
    )
```

```python
import functools

import jax
import jax.numpy as jnp
from jax import lax
from jax.experimental import pallas as pl
from jax.experimental.pallas import tpu as pltpu
from jax.sharding import PartitionSpec as P

EPS = 1e-05
MESH = pl.DeviceIdType.MESH
BF = jnp.bfloat16
F32 = jnp.float32
GROUPS = 8
SHARE = 48
ROWS = 384
WIDTH = 1024
LANES = 128
LOCAL_VARS = 6
LOADS = 12


def mm(a, b):
    return jnp.dot(a, b, preferred_element_type=F32)


def mm_nt(a, b):
    return lax.dot_general(a, b, (((1,), (1,)), ((), ())), preferred_element_type=F32)


def lane_of(shape):
    return lax.broadcasted_iota(jnp.int32, shape, len(shape) - 1)


def split_three(value):
    high = value.astype(BF).astype(F32)
    rest = value - high
    middle = rest.astype(BF).astype(F32)
    return high, middle, rest - middle


def layer_norm(values, gain):
    center = values - jnp.mean(values, axis=-1, keepdims=True)
    spread = jnp.mean(center * center, axis=-1, keepdims=True)
    return (center * lax.rsqrt(spread + EPS) * gain).astype(BF)


def kernel(
    fields,
    var_embed,
    pos_embed,
    agg_key,
    agg_query,
    agg_value,
    agg_out,
    gain_one,
    qkv_weight,
    attn_out,
    gain_two,
    mlp_in,
    mlp_out,
    out,
    field_s,
    embed_s,
    pos_s,
    key_s,
    query_s,
    value_s,
    aggout_s,
    gain1_s,
    qkv_s,
    attnout_s,
    gain2_s,
    mlpin_s,
    mlpout_s,
    kq_s,
    spread_s,
    pick_s,
    emb_s,
    weight_s,
    part_s,
    part_r,
    norm_r,
    q_s,
    qout_s,
    qin_r,
    kvout_s,
    kv_r,
    max_s,
    acc_s,
    att_s,
    att_r,
    upd_r,
    res_r,
    down_s,
    down_r,
    load_sem,
    field_sem,
    p1_send,
    p1_recv,
    p3_send,
    p3_recv,
    z_send,
    z_recv,
    kv_send,
    kv_recv,
    w_send,
    w_recv,
    v_send,
    v_recv,
    a_send,
    a_recv,
    p8_send,
    p8_recv,
    p10_send,
    p10_recv,
):
    tok = lax.axis_index("tok")
    me = lax.axis_index("var")
    core = lax.rem(tok, 2)
    half = tok // 8
    ring = lax.rem(tok // 2, 4)
    sibling = tok + 1 - 2 * core
    partner = tok + 8 - 16 * half

    def along_x(step):
        return half * 8 + lax.rem(ring + step, 4) * 2 + core

    plane = me // 4
    high_y = lax.rem(me, 4)

    def peer(step):
        return lax.rem(plane + 1 + step // 4, 2) * 4 + lax.rem(high_y + 3 - step % 4, 4)

    def remote(src, dst, send, recv, to_tok, to_var):
        return pltpu.make_async_remote_copy(
            src_ref=src,
            dst_ref=dst,
            send_sem=send,
            recv_sem=recv,
            device_id=(to_tok, to_var),
            device_id_type=MESH,
        )

    barrier = pltpu.get_barrier_semaphore()
    others = [(tok, peer(i)) for i in range(GROUPS - 1)]
    others += [(partner, lax.rem(me + i, GROUPS)) for i in range(GROUPS)]
    others += [(sibling, me)] + [(along_x(i), me) for i in (1, 2, 3)]
    for device in others:
        pl.semaphore_signal(barrier, inc=1, device_id=device, device_id_type=MESH)

    def field_copy(i):
        rows = pl.ds(pl.multiple_of(peer(i) * SHARE, 16), SHARE)
        return pltpu.make_async_copy(fields.at[:, rows, :], field_s.at[i], field_sem.at[i])

    own_rows = pl.ds(pl.multiple_of(me * SHARE, 16), SHARE)
    loads = [
        pltpu.make_async_copy(src, dst, load_sem.at[k])
        for k, (src, dst) in enumerate(
            [
                (agg_query, query_s),
                (var_embed, embed_s),
                (agg_key, key_s),
                (agg_value, value_s),
                (agg_out, aggout_s),
                (pos_embed.at[own_rows, :], pos_s),
                (gain_one, gain1_s),
                (qkv_weight, qkv_s),
                (attn_out.at[ring, core], attnout_s.at[me, ring, core]),
                (gain_two, gain2_s),
                (mlp_in, mlpin_s.at[0]),
                (mlp_out, mlpout_s.at[0]),
            ]
        )
    ]
    for k in (8, 0, 1, 2):
        loads[k].start()
    field_copy(0).start()
    loads[3].start()
    field_copy(1).start()

    row = lax.broadcasted_iota(jnp.int32, (LANES, WIDTH), 0)
    col = lax.broadcasted_iota(jnp.int32, (LANES, WIDTH), 1)
    spread_s[...] = jnp.where((row < 32) & (row % 16 == col // 64), 1.0, 0.0).astype(BF)
    row = lax.broadcasted_iota(jnp.int32, (LANES, LANES), 0)
    col = lax.broadcasted_iota(jnp.int32, (LANES, LANES), 1)
    same = row % 16 == col % 16
    pick_s[0] = jnp.where(same & (row < 48), 1.0, 0.0).astype(BF)
    pick_s[1] = jnp.where(same & (row >= 48) & (row < 96), 1.0, 0.0).astype(BF)

    loads[0].wait()
    heads = query_s[...]
    tiled = jnp.concatenate([heads] * 16, axis=1)
    row = lax.broadcasted_iota(jnp.int32, (16, WIDTH), 0)
    col = lax.broadcasted_iota(jnp.int32, (16, WIDTH), 1)
    tiled = jnp.where(col // 64 == row, tiled, 0.0)
    stacked = jnp.concatenate(split_three(tiled) + (jnp.zeros((80, WIDTH), F32),), axis=0)
    stacked = stacked.T.astype(BF)
    loads[2].wait()
    folded = mm(key_s[...], stacked)
    folded = folded + pltpu.roll(folded, 112, 1) + pltpu.roll(folded, 96, 1)
    folded = jnp.where(lane_of((WIDTH, LANES)) < 16, folded * 0.125, 0.0)
    for shift in (16, 32, 64):
        folded = folded + pltpu.roll(folded, shift, 1)
    kq_s[...] = folded.astype(BF)

    loads[1].wait()
    row = lax.broadcasted_iota(jnp.int32, (16, 48), 0)
    col = lax.broadcasted_iota(jnp.int32, (16, 48), 1)
    chosen = jnp.where((col == me * LOCAL_VARS + row) & (row < LOCAL_VARS), 1.0, 0.0).astype(BF)
    own_embed = mm(chosen, embed_s[...]).astype(BF)

    across = lax.rem(me + 4, GROUPS)
    mlp = (mlpin_s, mlpout_s)

    def w_copy(i, source):
        at = attnout_s.at[source, ring, core]
        return remote(at, at, w_send.at[i], w_recv.at[source], tok, peer(i))

    def mlp_copy(k):
        return remote(
            mlp[k].at[0, ring, core], mlp[k].at[1, ring, core], w_send.at[8 + k], w_recv.at[8 + k], tok, across
        )

    def spread_copy(k, step, place):
        at = attnout_s.at[:, place, core] if k == 2 else mlp[k].at[1, place, core]
        n = k * 3 + step - 1
        return remote(at, at, v_send.at[n], v_recv.at[n], along_x(step), me)

    def pair_copy(k, owner):
        at = attnout_s.at[:, :, owner] if k == 2 else mlp[k].at[1, :, owner]
        return remote(at, at, v_send.at[9 + k], v_recv.at[9 + k], sibling, me)

    def spread_arrived(k):
        for step in (1, 2, 3):
            spread_copy(k, step, lax.rem(ring + 4 - step, 4)).wait_recv()

    lane = lane_of((SHARE, LANES))

    def p1_copy(i, source):
        return remote(
            part_s.at[i], part_r.at[source], p1_send.at[i], p1_recv.at[source], tok, peer(i)
        )

    def weigh(i):
        at = i % 2
        for v in range(LOCAL_VARS):
            emb_s[at, v * SHARE : (v + 1) * SHARE, :] = field_s[i, v] + own_embed[v : v + 1, :]
        scores = mm(emb_s[at], kq_s[...]).reshape(LOCAL_VARS, SHARE, LANES)
        highest = jnp.max(scores, axis=0)
        expd = jnp.exp(scores - highest[None])
        totals = jnp.sum(expd, axis=0)
        coarse = expd.astype(BF).astype(F32)
        weights = jnp.where((lane < 16)[None], coarse, jnp.where((lane < 32)[None], expd - coarse, 0.0))
        weight_s[at] = weights.reshape(LOCAL_VARS * SHARE, LANES).astype(BF)
        high, middle, low = split_three(highest)
        high_t, middle_t, low_t = split_three(totals)
        notes = jnp.where(lane < 16, high, jnp.where(lane < 32, middle, low))
        notes_t = jnp.where(lane < 64, high_t, jnp.where(lane < 80, middle_t, low_t))
        part_s[i, :, WIDTH:] = jnp.where(lane < 48, notes, notes_t).astype(BF)

    def add_up(i):
        at = i % 2
        for n in range(2):
            cols = slice(n * 512, (n + 1) * 512)
            wide = mm(weight_s[at], spread_s[:, cols])
            projected = mm(emb_s[at], value_s[:, cols])
            term = (wide * projected).reshape(LOCAL_VARS, SHARE, 512)
            part_s[i, :, cols] = jnp.sum(term, axis=0).astype(BF)

    field_copy(0).wait()
    weigh(0)
    loads[3].wait()
    for i in range(GROUPS):
        if i + 2 < GROUPS:
            field_copy(i + 2).start()
        if i == 1:
            for k in (4, 5, 6, 7):
                loads[k].start()
        if i == 4:
            for k in (9, 10, 11):
                loads[k].start()
        if i + 1 < GROUPS:
            field_copy(i + 1).wait()
            weigh(i + 1)
        add_up(i)
        if i == 0:
            pl.semaphore_wait(barrier, len(others))
        if i < GROUPS - 1:
            p1_copy(i, me).start()
    loads[8].wait()
    for i in range(GROUPS - 1):
        w_copy(i, me).start()
    part_r[me] = part_s[GROUPS - 1]
    for i in range(GROUPS - 1):
        p1_copy(i, peer(i)).wait_recv()

    notes = part_r[:, :, WIDTH:].reshape(ROWS, LANES)
    highest = mm(notes, pick_s[0]).reshape(GROUPS, SHARE, LANES)
    totals = mm(notes, pick_s[1]).reshape(GROUPS, SHARE, LANES)
    scale = jnp.exp(highest - jnp.max(highest, axis=0)[None])
    scale = scale / jnp.sum(scale * totals, axis=0)[None]
    coarse = scale.astype(BF).astype(F32)
    scale = jnp.where((lane < 16)[None], coarse, jnp.where((lane < 32)[None], scale - coarse, 0.0))
    scale = scale.reshape(ROWS, LANES).astype(BF)
    mixed = []
    for n in range(4):
        cols = slice(n * 256, (n + 1) * 256)
        wide = mm(scale, spread_s[:, cols]).reshape(GROUPS, SHARE, 256)
        mixed.append(jnp.sum(wide * part_r[:, :, cols].astype(F32), axis=0).astype(BF))
    mixed = jnp.concatenate(mixed, axis=1)
    for k in (4, 5, 6):
        loads[k].wait()
    stream = (mm(mixed, aggout_s[...]) + pos_s[...].astype(F32)).astype(BF)
    norm_r[me] = layer_norm(stream.astype(F32), gain1_s[...])

    def gather_copy(buffer, send, recv, i, source):
        return remote(buffer.at[source], buffer.at[source], send.at[i], recv.at[source], tok, peer(i))

    for i in range(GROUPS - 1):
        gather_copy(norm_r, p3_send, p3_recv, i, me).start()
    loads[7].wait()
    for i in range(GROUPS - 1):
        w_copy(i, peer(i)).wait_recv()
    for step in (1, 2, 3):
        spread_copy(2, step, ring).start()
    for i in range(GROUPS - 1):
        gather_copy(norm_r, p3_send, p3_recv, i, peer(i)).wait_recv()

    normed = norm_r[...].reshape(ROWS, WIDTH)
    keys = mm(normed, qkv_s[1])
    values = mm(normed, qkv_s[2])
    wide_lane = lane_of((ROWS, LANES))
    left = wide_lane < 64
    kv_a = jnp.where(left, keys, pltpu.roll(values, 64, 1)).astype(BF)
    kv_b = jnp.where(left, pltpu.roll(keys, 64, 1), values).astype(BF)
    first = half == 0
    kv_r[core] = jnp.where(first, kv_a, kv_b)
    kvout_s[...] = jnp.where(first, kv_b, kv_a)

    def slot(order, owner):
        return order * 2 + owner

    z_kv = remote(kvout_s, kv_r.at[slot(1, core)], z_send.at[0], kv_recv.at[slot(1, core)], partner, me)
    z_kv.start()
    hops = ((2, 3), (3, 1), (4, 2))

    def x_copy(k, order, source):
        to = slot(order, core)
        return remote(
            kv_r.at[source], kv_r.at[to], kv_send.at[k], kv_recv.at[to], along_x(hops[k % 3][1]), me
        )

    for k in range(3):
        x_copy(k, hops[k][0], slot(0, core)).start()

    def share_copy(order, owner):
        at = slot(order, owner)
        return remote(kv_r.at[at], kv_r.at[at], kv_send.at[8 + order], kv_recv.at[at], sibling, me)

    share_copy(0, core).start()
    queries = mm(normed, qkv_s[0]) * 0.125
    rolled = pltpu.roll(queries, 64, 1)
    q_a = jnp.where(left, queries, 0.0).astype(BF)
    q_b = jnp.where(left, rolled, 0.0).astype(BF)
    q_s[0:ROWS, :] = jnp.where(first, q_a, q_b)
    other = jnp.where(first, rolled, queries)
    qout_s[...] = jnp.where(
        left[: ROWS // 2], other[: ROWS // 2], pltpu.roll(other[ROWS // 2 :], 64, 1)
    ).astype(BF)
    z_q = remote(qout_s, qin_r, z_send.at[1], z_recv.at[0], partner, me)
    z_q.start()
    for k in (10, 11):
        loads[k].wait()
    for k in range(2):
        mlp_copy(k).start()

    spread_arrived(2)
    pair_copy(2, core).start()
    max_s[...] = jnp.full(max_s.shape, -jnp.inf, F32)
    acc_s[...] = jnp.zeros(acc_s.shape, F32)
    z_kv.wait_recv()
    for k in range(3):
        x_copy(3 + k, hops[k][0] + 3, slot(1, core)).start()
    z_q.wait_recv()
    packed = qin_r[...].astype(F32)
    q_s[ROWS : ROWS + ROWS // 2, :] = jnp.where(left[: ROWS // 2], packed, 0.0).astype(BF)
    q_s[ROWS + ROWS // 2 :, :] = jnp.where(
        left[: ROWS // 2], pltpu.roll(packed, 64, 1), 0.0
    ).astype(BF)

    def pass_on(order):
        share_copy(order, core).wait_recv()
        share_copy(order, core).start()

    share_copy(1, core).start()
    pass_on(2)
    pass_on(3)
    many_left = lane_of((4 * ROWS, LANES)) < 64

    def attend_step(step, carry):
        @pl.when(step == 1)
        def _():
            pass_on(4)

        @pl.when(step == 2)
        def _():
            pass_on(5)
            pass_on(6)

        @pl.when(step == 3)
        def _():
            pass_on(7)
            for k in range(2):
                mlp_copy(k).wait_recv()
                for hop in (1, 2, 3):
                    spread_copy(k, hop, ring).start()

        for order in (2 * step, 2 * step + 1):
            share_copy(order, 1 - core).wait_recv()
        block = kv_r[pl.ds(step * 4, 4)].reshape(4 * ROWS, LANES)
        ones = jnp.where(many_left, 1.0, block.astype(F32)).astype(BF)
        logits = mm_nt(q_s[...], block)
        before = max_s[...]
        newest = jnp.maximum(before, jnp.max(logits, axis=1, keepdims=True))
        probs = jnp.exp(logits - jnp.concatenate([newest] * 12, axis=1)).astype(BF)
        acc_s[...] = acc_s[...] * jnp.exp(before - newest) + mm(probs, ones)
        max_s[...] = newest
        return carry

    lax.fori_loop(0, 4, attend_step, 0)

    acc = acc_s[...]
    turned = pltpu.roll(acc, 64, 1)
    wide_left = lane_of((2 * ROWS, LANES)) < 64
    result = jnp.where(wide_left, turned, acc) / jnp.where(wide_left, acc, turned)
    keep = wide_left == jnp.broadcast_to(first, wide_left.shape)
    att_s[...] = jnp.where(keep, result, 0.0).astype(BF).reshape(2, GROUPS, SHARE, LANES)
    att_r[half, me] = att_s[0, me]

    def att_copy(side, i, at, source):
        to = peer(i)
        return remote(
            att_s.at[side, to],
            att_r.at[at, source],
            a_send.at[side * GROUPS + i],
            a_recv.at[at * GROUPS + source],
            tok if side == 0 else partner,
            to,
        )

    for i in range(GROUPS - 1):
        att_copy(0, i, half, me).start()
        att_copy(1, i, half, me).start()
    att_copy(1, GROUPS - 1, half, me).start()

    for i in range(GROUPS - 1):
        att_copy(0, i, half, peer(i)).wait_recv()
    for i in range(GROUPS):
        att_copy(1, i, 1 - half, peer(i)).wait_recv()

    pair_copy(2, 1 - core).wait_recv()
    attended = jnp.concatenate([att_r[0, g] + att_r[1, g] for g in range(GROUPS)], axis=1)
    attn_sum = mm(attended, attnout_s[...].reshape(WIDTH, WIDTH))
    def along_y(i):
        return lax.rem(high_y + 1 + i, 4)

    def upd_copy(i, source):
        at = upd_r.at[source]
        return remote(at, at, p8_send.at[i], p8_recv.at[source], tok, plane * 4 + along_y(i))

    def res_copy(i, source):
        to = (1 - plane) * 4 + i
        cols = pl.ds(pl.multiple_of(to * LANES, LANES), LANES)
        return remote(
            upd_r.at[high_y, :, cols], res_r.at[source], p8_send.at[4 + i], p8_recv.at[4 + source], tok, to
        )

    upd_r[high_y] = (stream.astype(F32) + attn_sum).astype(BF)
    for i in range(3):
        upd_copy(i, high_y).start()
    for i in range(4):
        res_copy(i, high_y).start()
    loads[9].wait()
    for k in range(2):
        spread_arrived(k)
        pair_copy(k, core).start()
    for i in range(3):
        upd_copy(i, along_y(i)).wait_recv()

    updated = upd_r[...].reshape(ROWS // 2, WIDTH)
    normed_two = layer_norm(updated.astype(F32), gain2_s[...])
    for k in range(2):
        pair_copy(k, 1 - core).wait_recv()
    hidden = []
    for k in range(2):
        raised = mm(normed_two, mlpin_s[k].reshape(WIDTH, 512))
        hidden.append((0.5 * raised * (1.0 + lax.erf(raised * 0.7071067811865476))).astype(BF))
    hidden = jnp.concatenate(hidden, axis=1)
    down_weight = mlpout_s[...].reshape(WIDTH, WIDTH)
    for n in range(4):
        terms = mm(hidden, down_weight[:, n * 256 : (n + 1) * 256]).astype(BF)
        down_s[2 * n] = terms[:, :LANES]
        down_s[2 * n + 1] = terms[:, LANES:]

    def down_copy(i, source):
        return remote(
            down_s.at[peer(i)],
            down_r.at[source],
            p10_send.at[i],
            p10_recv.at[source],
            tok,
            peer(i),
        )

    for i in range(GROUPS - 1):
        down_copy(i, me).start()
    down_r[me] = down_s[me]
    own_cols = pl.ds(pl.multiple_of(me * LANES, LANES), LANES)
    for i in range(4):
        res_copy(i, i).wait_recv()
    for i in range(GROUPS - 1):
        down_copy(i, peer(i)).wait_recv()

    def finish_half(which, residual):
        terms = jnp.sum(down_r[pl.ds(which * 4, 4)].astype(F32), axis=0)
        rows = pl.ds(pl.multiple_of(which * (ROWS // 2), 16), ROWS // 2)
        out[rows, :] = (residual.reshape(ROWS // 2, LANES).astype(F32) + terms).astype(BF)

    finish_half(plane, upd_r[:, :, own_cols])
    finish_half(1 - plane, res_r[...])

    for i in range(GROUPS - 1):
        p1_copy(i, me).wait_send()
        gather_copy(norm_r, p3_send, p3_recv, i, me).wait_send()
        w_copy(i, me).wait_send()
        att_copy(0, i, half, me).wait_send()
        down_copy(i, me).wait_send()
    for i in range(GROUPS):
        att_copy(1, i, half, me).wait_send()
        share_copy(i, core).wait_send()
    for k in range(3):
        x_copy(k, hops[k][0], slot(0, core)).wait_send()
        x_copy(3 + k, hops[k][0] + 3, slot(1, core)).wait_send()
    z_kv.wait_send()
    z_q.wait_send()
    for i in range(3):
        upd_copy(i, high_y).wait_send()
        pair_copy(i, core).wait_send()
        for step in (1, 2, 3):
            spread_copy(i, step, ring).wait_send()
    for i in range(4):
        res_copy(i, high_y).wait_send()
    for k in range(2):
        mlp_copy(k).wait_send()


def scratch():
    vmem = pltpu.VMEM
    dma = pltpu.SemaphoreType.DMA
    return [
        vmem((GROUPS, LOCAL_VARS, SHARE, WIDTH), BF),
        vmem((48, WIDTH), BF),
        vmem((SHARE, WIDTH), BF),
        vmem((WIDTH, WIDTH), BF),
        vmem((16, 64), F32),
        vmem((WIDTH, WIDTH), BF),
        vmem((WIDTH, WIDTH), BF),
        vmem((1, WIDTH), F32),
        vmem((3, WIDTH, LANES), BF),
        vmem((GROUPS, 4, 2, 16, WIDTH), BF),
        vmem((1, WIDTH), F32),
        vmem((2, 4, 2, LANES, 512), BF),
        vmem((2, 4, 2, 64, WIDTH), BF),
        vmem((WIDTH, LANES), BF),
        vmem((LANES, WIDTH), BF),
        vmem((2, LANES, LANES), BF),
        vmem((2, LOCAL_VARS * SHARE, WIDTH), BF),
        vmem((2, LOCAL_VARS * SHARE, LANES), BF),
        vmem((GROUPS, SHARE, WIDTH + LANES), BF),
        vmem((GROUPS, SHARE, WIDTH + LANES), BF),
        vmem((GROUPS, SHARE, WIDTH), BF),
        vmem((2 * ROWS, LANES), BF),
        vmem((ROWS // 2, LANES), BF),
        vmem((ROWS // 2, LANES), BF),
        vmem((ROWS, LANES), BF),
        vmem((16, ROWS, LANES), BF),
        vmem((2 * ROWS, LANES), F32),
        vmem((2 * ROWS, LANES), F32),
        vmem((2, GROUPS, SHARE, LANES), BF),
        vmem((2, GROUPS, SHARE, LANES), BF),
        vmem((4, SHARE, WIDTH), BF),
        vmem((4, SHARE, LANES), BF),
        vmem((GROUPS, ROWS // 2, LANES), BF),
        vmem((GROUPS, ROWS // 2, LANES), BF),
        dma((LOADS,)),
        dma((GROUPS,)),
        dma((GROUPS,)),
        dma((GROUPS,)),
        dma((GROUPS,)),
        dma((GROUPS,)),
        dma((2,)),
        dma((1,)),
        dma((16,)),
        dma((16,)),
        dma((12,)),
        dma((12,)),
        dma((2 * GROUPS,)),
        dma((2 * GROUPS,)),
        dma((2 * GROUPS,)),
        dma((2 * GROUPS,)),
        dma((GROUPS,)),
        dma((GROUPS,)),
        dma((GROUPS,)),
        dma((GROUPS,)),
    ]


def body(
    fields,
    var_embed,
    pos_embed,
    agg_key,
    agg_query,
    agg_value,
    agg_out,
    gain_one,
    qkv_weight,
    attn_out,
    gain_two,
    mlp_in,
    mlp_out,
):
    return pl.pallas_call(
        kernel,
        out_shape=jax.ShapeDtypeStruct((ROWS, LANES), BF),
        in_specs=[pl.BlockSpec(memory_space=pl.ANY)] * 13,
        out_specs=pl.BlockSpec(memory_space=pltpu.VMEM),
        scratch_shapes=scratch(),
        compiler_params=pltpu.CompilerParams(
            collective_id=0, has_side_effects=True, vmem_limit_bytes=56 * 2**20
        ),
    )(
        fields,
        var_embed,
        pos_embed,
        agg_key,
        agg_query,
        agg_value,
        agg_out,
        gain_one.reshape(1, WIDTH),
        qkv_weight,
        attn_out.reshape(4, 2, 16, WIDTH),
        gain_two.reshape(1, WIDTH),
        mlp_in.reshape(4, 2, LANES, 512),
        mlp_out.reshape(4, 2, 64, WIDTH),
    )


def solution(mesh):
    placed = (
        P("var", "tok", None),
        P(),
        P("tok", None),
        P(),
        P(),
        P(),
        P(),
        P(),
        P(None, None, "var"),
        P("var", None),
        P(),
        P(None, "var"),
        P("var", None),
    )
    return jax.shard_map(
        body, mesh=mesh, in_specs=placed, out_specs=P("tok", "var"), check_vma=False
    )
```

```python
import functools

import jax
import jax.numpy as jnp
from jax import lax
from jax.experimental import pallas as pl
from jax.experimental.pallas import tpu as pltpu
from jax.sharding import PartitionSpec as P

EPS = 1e-05
MESH = pl.DeviceIdType.MESH
BF = jnp.bfloat16
F32 = jnp.float32
GROUPS = 8
SHARE = 48
ROWS = 384
WIDTH = 1024
LANES = 128
LOCAL_VARS = 6
LOADS = 12


def mm(a, b):
    return jnp.dot(a, b, preferred_element_type=F32)


def mm_nt(a, b):
    return lax.dot_general(a, b, (((1,), (1,)), ((), ())), preferred_element_type=F32)


def lane_of(shape):
    return lax.broadcasted_iota(jnp.int32, shape, len(shape) - 1)


def split_three(value):
    high = value.astype(BF).astype(F32)
    rest = value - high
    middle = rest.astype(BF).astype(F32)
    return high, middle, rest - middle


def layer_norm(values, gain):
    center = values - jnp.mean(values, axis=-1, keepdims=True)
    spread = jnp.mean(center * center, axis=-1, keepdims=True)
    return (center * lax.rsqrt(spread + EPS) * gain).astype(BF)


def kernel(
    fields,
    var_embed,
    pos_embed,
    agg_key,
    agg_query,
    agg_value,
    agg_out,
    gain_one,
    qkv_weight,
    attn_out,
    gain_two,
    mlp_in,
    mlp_out,
    out,
    field_s,
    embed_s,
    pos_s,
    key_s,
    query_s,
    value_s,
    aggout_s,
    gain1_s,
    qkv_s,
    attnout_s,
    gain2_s,
    mlpin_s,
    mlpout_s,
    kq_s,
    spread_s,
    pick_s,
    emb_s,
    weight_s,
    part_s,
    part_r,
    norm_r,
    q_s,
    qout_s,
    qin_r,
    kvout_s,
    kv_r,
    max_s,
    acc_s,
    att_s,
    att_r,
    upd_r,
    res_r,
    down_s,
    down_r,
    load_sem,
    field_sem,
    p1_send,
    p1_recv,
    p3_send,
    p3_recv,
    z_send,
    z_recv,
    kv_send,
    kv_recv,
    w_send,
    w_recv,
    v_send,
    v_recv,
    a_send,
    a_recv,
    p8_send,
    p8_recv,
    p10_send,
    p10_recv,
):
    tok = lax.axis_index("tok")
    me = lax.axis_index("var")
    core = lax.rem(tok, 2)
    half = tok // 8
    ring = lax.rem(tok // 2, 4)
    sibling = tok + 1 - 2 * core
    partner = tok + 8 - 16 * half

    def along_x(step):
        return half * 8 + lax.rem(ring + step, 4) * 2 + core

    plane = me // 4
    high_y = lax.rem(me, 4)

    def peer(step):
        return lax.rem(plane + 1 + step // 4, 2) * 4 + lax.rem(high_y + 3 - step % 4, 4)

    def remote(src, dst, send, recv, to_tok, to_var):
        return pltpu.make_async_remote_copy(
            src_ref=src,
            dst_ref=dst,
            send_sem=send,
            recv_sem=recv,
            device_id=(to_tok, to_var),
            device_id_type=MESH,
        )

    barrier = pltpu.get_barrier_semaphore()
    others = [(tok, peer(i)) for i in range(GROUPS - 1)]
    others += [(partner, lax.rem(me + i, GROUPS)) for i in range(GROUPS)]
    others += [(sibling, me)] + [(along_x(i), me) for i in (1, 2, 3)]
    for device in others:
        pl.semaphore_signal(barrier, inc=1, device_id=device, device_id_type=MESH)

    def field_copy(i):
        rows = pl.ds(pl.multiple_of(peer(i) * SHARE, 16), SHARE)
        return pltpu.make_async_copy(fields.at[:, rows, :], field_s.at[i], field_sem.at[i])

    own_rows = pl.ds(pl.multiple_of(me * SHARE, 16), SHARE)
    loads = [
        pltpu.make_async_copy(src, dst, load_sem.at[k])
        for k, (src, dst) in enumerate(
            [
                (agg_query, query_s),
                (var_embed, embed_s),
                (agg_key, key_s),
                (agg_value, value_s),
                (agg_out, aggout_s),
                (pos_embed.at[own_rows, :], pos_s),
                (gain_one, gain1_s),
                (qkv_weight, qkv_s),
                (attn_out.at[ring, core], attnout_s.at[me, ring, core]),
                (gain_two, gain2_s),
                (mlp_in, mlpin_s.at[0]),
                (mlp_out, mlpout_s.at[0]),
            ]
        )
    ]
    for k in (8, 0, 1, 2):
        loads[k].start()
    field_copy(0).start()
    loads[3].start()
    field_copy(1).start()

    row = lax.broadcasted_iota(jnp.int32, (LANES, WIDTH), 0)
    col = lax.broadcasted_iota(jnp.int32, (LANES, WIDTH), 1)
    spread_s[...] = jnp.where((row < 32) & (row % 16 == col // 64), 1.0, 0.0).astype(BF)
    row = lax.broadcasted_iota(jnp.int32, (LANES, LANES), 0)
    col = lax.broadcasted_iota(jnp.int32, (LANES, LANES), 1)
    same = row % 16 == col % 16
    pick_s[0] = jnp.where(same & (row < 48), 1.0, 0.0).astype(BF)
    pick_s[1] = jnp.where(same & (row >= 48) & (row < 96), 1.0, 0.0).astype(BF)

    loads[0].wait()
    heads = query_s[...]
    tiled = jnp.concatenate([heads] * 16, axis=1)
    row = lax.broadcasted_iota(jnp.int32, (16, WIDTH), 0)
    col = lax.broadcasted_iota(jnp.int32, (16, WIDTH), 1)
    tiled = jnp.where(col // 64 == row, tiled, 0.0)
    stacked = jnp.concatenate(split_three(tiled) + (jnp.zeros((80, WIDTH), F32),), axis=0)
    stacked = stacked.T.astype(BF)
    loads[2].wait()
    folded = mm(key_s[...], stacked)
    folded = folded + pltpu.roll(folded, 112, 1) + pltpu.roll(folded, 96, 1)
    folded = jnp.where(lane_of((WIDTH, LANES)) < 16, folded * 0.125, 0.0)
    for shift in (16, 32, 64):
        folded = folded + pltpu.roll(folded, shift, 1)
    kq_s[...] = folded.astype(BF)

    loads[1].wait()
    row = lax.broadcasted_iota(jnp.int32, (16, 48), 0)
    col = lax.broadcasted_iota(jnp.int32, (16, 48), 1)
    chosen = jnp.where((col == me * LOCAL_VARS + row) & (row < LOCAL_VARS), 1.0, 0.0).astype(BF)
    own_embed = mm(chosen, embed_s[...]).astype(BF)

    across = lax.rem(me + 4, GROUPS)
    mlp = (mlpin_s, mlpout_s)

    def w_copy(i, source):
        at = attnout_s.at[source, ring, core]
        return remote(at, at, w_send.at[i], w_recv.at[source], tok, peer(i))

    def mlp_copy(k):
        return remote(
            mlp[k].at[0, ring, core], mlp[k].at[1, ring, core], w_send.at[8 + k], w_recv.at[8 + k], tok, across
        )

    def spread_copy(k, step, place):
        at = attnout_s.at[:, place, core] if k == 2 else mlp[k].at[1, place, core]
        n = k * 3 + step - 1
        return remote(at, at, v_send.at[n], v_recv.at[n], along_x(step), me)

    def pair_copy(k, owner):
        at = attnout_s.at[:, :, owner] if k == 2 else mlp[k].at[1, :, owner]
        return remote(at, at, v_send.at[9 + k], v_recv.at[9 + k], sibling, me)

    def spread_arrived(k):
        for step in (1, 2, 3):
            spread_copy(k, step, lax.rem(ring + 4 - step, 4)).wait_recv()

    lane = lane_of((SHARE, LANES))

    def p1_copy(i, source):
        return remote(
            part_s.at[i], part_r.at[source], p1_send.at[i], p1_recv.at[source], tok, peer(i)
        )

    def weigh(i):
        at = i % 2
        for v in range(LOCAL_VARS):
            emb_s[at, v * SHARE : (v + 1) * SHARE, :] = field_s[i, v] + own_embed[v : v + 1, :]
        scores = mm(emb_s[at], kq_s[...]).reshape(LOCAL_VARS, SHARE, LANES)
        highest = jnp.max(scores, axis=0)
        expd = jnp.exp(scores - highest[None])
        totals = jnp.sum(expd, axis=0)
        coarse = expd.astype(BF).astype(F32)
        weights = jnp.where((lane < 16)[None], coarse, jnp.where((lane < 32)[None], expd - coarse, 0.0))
        weight_s[at] = weights.reshape(LOCAL_VARS * SHARE, LANES).astype(BF)
        high, middle, low = split_three(highest)
        high_t, middle_t, low_t = split_three(totals)
        notes = jnp.where(lane < 16, high, jnp.where(lane < 32, middle, low))
        notes_t = jnp.where(lane < 64, high_t, jnp.where(lane < 80, middle_t, low_t))
        part_s[i, :, WIDTH:] = jnp.where(lane < 48, notes, notes_t).astype(BF)

    def add_up(i):
        at = i % 2
        for n in range(2):
            cols = slice(n * 512, (n + 1) * 512)
            wide = mm(weight_s[at], spread_s[:, cols])
            projected = mm(emb_s[at], value_s[:, cols])
            term = (wide * projected).reshape(LOCAL_VARS, SHARE, 512)
            part_s[i, :, cols] = jnp.sum(term, axis=0).astype(BF)

    field_copy(0).wait()
    weigh(0)
    loads[3].wait()
    for i in range(GROUPS):
        if i + 2 < GROUPS:
            field_copy(i + 2).start()
        if i == 1:
            for k in (4, 5, 6, 7):
                loads[k].start()
        if i == 4:
            for k in (9, 10, 11):
                loads[k].start()
        if i + 1 < GROUPS:
            field_copy(i + 1).wait()
            weigh(i + 1)
        add_up(i)
        if i == 0:
            pl.semaphore_wait(barrier, len(others))
        if i < GROUPS - 1:
            p1_copy(i, me).start()
    loads[8].wait()
    for i in range(GROUPS - 1):
        w_copy(i, me).start()
    part_r[me] = part_s[GROUPS - 1]
    for i in range(GROUPS - 1):
        p1_copy(i, peer(i)).wait_recv()

    notes = part_r[:, :, WIDTH:].reshape(ROWS, LANES)
    highest = mm(notes, pick_s[0]).reshape(GROUPS, SHARE, LANES)
    totals = mm(notes, pick_s[1]).reshape(GROUPS, SHARE, LANES)
    scale = jnp.exp(highest - jnp.max(highest, axis=0)[None])
    scale = scale / jnp.sum(scale * totals, axis=0)[None]
    coarse = scale.astype(BF).astype(F32)
    scale = jnp.where((lane < 16)[None], coarse, jnp.where((lane < 32)[None], scale - coarse, 0.0))
    scale = scale.reshape(ROWS, LANES).astype(BF)
    mixed = []
    for n in range(4):
        cols = slice(n * 256, (n + 1) * 256)
        wide = mm(scale, spread_s[:, cols]).reshape(GROUPS, SHARE, 256)
        mixed.append(jnp.sum(wide * part_r[:, :, cols].astype(F32), axis=0).astype(BF))
    mixed = jnp.concatenate(mixed, axis=1)
    for k in (4, 5, 6):
        loads[k].wait()
    stream = (mm(mixed, aggout_s[...]) + pos_s[...].astype(F32)).astype(BF)
    norm_r[me] = layer_norm(stream.astype(F32), gain1_s[...])

    def gather_copy(buffer, send, recv, i, source):
        return remote(buffer.at[source], buffer.at[source], send.at[i], recv.at[source], tok, peer(i))

    for i in range(GROUPS - 1):
        gather_copy(norm_r, p3_send, p3_recv, i, me).start()
    for k in (10, 11):
        loads[k].wait()
    for k in range(2):
        mlp_copy(k).start()
    loads[7].wait()
    for i in range(GROUPS - 1):
        w_copy(i, peer(i)).wait_recv()
    for step in (1, 2, 3):
        spread_copy(2, step, ring).start()
    for i in range(GROUPS - 1):
        gather_copy(norm_r, p3_send, p3_recv, i, peer(i)).wait_recv()

    normed = norm_r[...].reshape(ROWS, WIDTH)
    keys = mm(normed, qkv_s[1])
    values = mm(normed, qkv_s[2])
    wide_lane = lane_of((ROWS, LANES))
    left = wide_lane < 64
    kv_a = jnp.where(left, keys, pltpu.roll(values, 64, 1)).astype(BF)
    kv_b = jnp.where(left, pltpu.roll(keys, 64, 1), values).astype(BF)
    first = half == 0
    kv_r[core] = jnp.where(first, kv_a, kv_b)
    kvout_s[...] = jnp.where(first, kv_b, kv_a)

    def slot(order, owner):
        return order * 2 + owner

    z_kv = remote(kvout_s, kv_r.at[slot(1, core)], z_send.at[0], kv_recv.at[slot(1, core)], partner, me)
    z_kv.start()
    hops = ((2, 3), (3, 1), (4, 2))

    def x_copy(k, order, source):
        to = slot(order, core)
        return remote(
            kv_r.at[source], kv_r.at[to], kv_send.at[k], kv_recv.at[to], along_x(hops[k % 3][1]), me
        )

    for k in range(3):
        x_copy(k, hops[k][0], slot(0, core)).start()

    def share_copy(order, owner):
        at = slot(order, owner)
        return remote(kv_r.at[at], kv_r.at[at], kv_send.at[8 + order], kv_recv.at[at], sibling, me)

    share_copy(0, core).start()
    queries = mm(normed, qkv_s[0]) * 0.125
    rolled = pltpu.roll(queries, 64, 1)
    q_a = jnp.where(left, queries, 0.0).astype(BF)
    q_b = jnp.where(left, rolled, 0.0).astype(BF)
    q_s[0:ROWS, :] = jnp.where(first, q_a, q_b)
    other = jnp.where(first, rolled, queries)
    qout_s[...] = jnp.where(
        left[: ROWS // 2], other[: ROWS // 2], pltpu.roll(other[ROWS // 2 :], 64, 1)
    ).astype(BF)
    z_q = remote(qout_s, qin_r, z_send.at[1], z_recv.at[0], partner, me)
    z_q.start()

    spread_arrived(2)
    pair_copy(2, core).start()
    max_s[...] = jnp.full(max_s.shape, -jnp.inf, F32)
    acc_s[...] = jnp.zeros(acc_s.shape, F32)
    z_kv.wait_recv()
    for k in range(3):
        x_copy(3 + k, hops[k][0] + 3, slot(1, core)).start()
    z_q.wait_recv()
    packed = qin_r[...].astype(F32)
    q_s[ROWS : ROWS + ROWS // 2, :] = jnp.where(left[: ROWS // 2], packed, 0.0).astype(BF)
    q_s[ROWS + ROWS // 2 :, :] = jnp.where(
        left[: ROWS // 2], pltpu.roll(packed, 64, 1), 0.0
    ).astype(BF)

    def pass_on(order):
        share_copy(order, core).wait_recv()
        share_copy(order, core).start()

    share_copy(1, core).start()
    pass_on(2)
    pass_on(3)
    many_left = lane_of((4 * ROWS, LANES)) < 64

    def attend_step(step, carry):
        @pl.when(step == 1)
        def _():
            pass_on(4)

        @pl.when(step == 2)
        def _():
            for k in range(2):
                mlp_copy(k).wait_recv()
                for hop in (1, 2, 3):
                    spread_copy(k, hop, ring).start()
            pass_on(5)
            pass_on(6)

        @pl.when(step == 3)
        def _():
            pass_on(7)

        for order in (2 * step, 2 * step + 1):
            share_copy(order, 1 - core).wait_recv()
        block = kv_r[pl.ds(step * 4, 4)].reshape(4 * ROWS, LANES)
        ones = jnp.where(many_left, 1.0, block.astype(F32)).astype(BF)
        logits = mm_nt(q_s[...], block)
        before = max_s[...]
        newest = jnp.maximum(before, jnp.max(logits, axis=1, keepdims=True))
        probs = jnp.exp(logits - jnp.concatenate([newest] * 12, axis=1)).astype(BF)
        acc_s[...] = acc_s[...] * jnp.exp(before - newest) + mm(probs, ones)
        max_s[...] = newest
        return carry

    lax.fori_loop(0, 4, attend_step, 0)

    acc = acc_s[...]
    turned = pltpu.roll(acc, 64, 1)
    wide_left = lane_of((2 * ROWS, LANES)) < 64
    result = jnp.where(wide_left, turned, acc) / jnp.where(wide_left, acc, turned)
    keep = wide_left == jnp.broadcast_to(first, wide_left.shape)
    att_s[...] = jnp.where(keep, result, 0.0).astype(BF).reshape(2, GROUPS, SHARE, LANES)
    att_r[half, me] = att_s[0, me]

    def att_copy(side, i, at, source):
        to = peer(i)
        return remote(
            att_s.at[side, to],
            att_r.at[at, source],
            a_send.at[side * GROUPS + i],
            a_recv.at[at * GROUPS + source],
            tok if side == 0 else partner,
            to,
        )

    for i in range(GROUPS - 1):
        att_copy(0, i, half, me).start()
        att_copy(1, i, half, me).start()
    att_copy(1, GROUPS - 1, half, me).start()

    for i in range(GROUPS - 1):
        att_copy(0, i, half, peer(i)).wait_recv()
    for i in range(GROUPS):
        att_copy(1, i, 1 - half, peer(i)).wait_recv()

    pair_copy(2, 1 - core).wait_recv()
    attended = jnp.concatenate([att_r[0, g] + att_r[1, g] for g in range(GROUPS)], axis=1)
    attn_sum = mm(attended, attnout_s[...].reshape(WIDTH, WIDTH))
    def along_y(i):
        return lax.rem(high_y + 1 + i, 4)

    def upd_copy(i, source):
        at = upd_r.at[source]
        return remote(at, at, p8_send.at[i], p8_recv.at[source], tok, plane * 4 + along_y(i))

    def res_copy(i, source):
        to = (1 - plane) * 4 + i
        cols = pl.ds(pl.multiple_of(to * LANES, LANES), LANES)
        return remote(
            upd_r.at[high_y, :, cols], res_r.at[source], p8_send.at[4 + i], p8_recv.at[4 + source], tok, to
        )

    upd_r[high_y] = (stream.astype(F32) + attn_sum).astype(BF)
    for i in range(3):
        upd_copy(i, high_y).start()
    for i in range(4):
        res_copy(i, high_y).start()
    loads[9].wait()
    for k in range(2):
        spread_arrived(k)
        pair_copy(k, core).start()
    for i in range(3):
        upd_copy(i, along_y(i)).wait_recv()

    updated = upd_r[...].reshape(ROWS // 2, WIDTH)
    normed_two = layer_norm(updated.astype(F32), gain2_s[...])
    for k in range(2):
        pair_copy(k, 1 - core).wait_recv()
    hidden = []
    for k in range(2):
        raised = mm(normed_two, mlpin_s[k].reshape(WIDTH, 512))
        hidden.append((0.5 * raised * (1.0 + lax.erf(raised * 0.7071067811865476))).astype(BF))
    hidden = jnp.concatenate(hidden, axis=1)
    down_weight = mlpout_s[...].reshape(WIDTH, WIDTH)
    for n in range(4):
        terms = mm(hidden, down_weight[:, n * 256 : (n + 1) * 256]).astype(BF)
        down_s[2 * n] = terms[:, :LANES]
        down_s[2 * n + 1] = terms[:, LANES:]

    def down_copy(i, source):
        return remote(
            down_s.at[peer(i)],
            down_r.at[source],
            p10_send.at[i],
            p10_recv.at[source],
            tok,
            peer(i),
        )

    for i in range(GROUPS - 1):
        down_copy(i, me).start()
    down_r[me] = down_s[me]
    own_cols = pl.ds(pl.multiple_of(me * LANES, LANES), LANES)
    for i in range(4):
        res_copy(i, i).wait_recv()
    for i in range(GROUPS - 1):
        down_copy(i, peer(i)).wait_recv()

    def finish_half(which, residual):
        terms = jnp.sum(down_r[pl.ds(which * 4, 4)].astype(F32), axis=0)
        rows = pl.ds(pl.multiple_of(which * (ROWS // 2), 16), ROWS // 2)
        out[rows, :] = (residual.reshape(ROWS // 2, LANES).astype(F32) + terms).astype(BF)

    finish_half(plane, upd_r[:, :, own_cols])
    finish_half(1 - plane, res_r[...])

    for i in range(GROUPS - 1):
        p1_copy(i, me).wait_send()
        gather_copy(norm_r, p3_send, p3_recv, i, me).wait_send()
        w_copy(i, me).wait_send()
        att_copy(0, i, half, me).wait_send()
        down_copy(i, me).wait_send()
    for i in range(GROUPS):
        att_copy(1, i, half, me).wait_send()
        share_copy(i, core).wait_send()
    for k in range(3):
        x_copy(k, hops[k][0], slot(0, core)).wait_send()
        x_copy(3 + k, hops[k][0] + 3, slot(1, core)).wait_send()
    z_kv.wait_send()
    z_q.wait_send()
    for i in range(3):
        upd_copy(i, high_y).wait_send()
        pair_copy(i, core).wait_send()
        for step in (1, 2, 3):
            spread_copy(i, step, ring).wait_send()
    for i in range(4):
        res_copy(i, high_y).wait_send()
    for k in range(2):
        mlp_copy(k).wait_send()


def scratch():
    vmem = pltpu.VMEM
    dma = pltpu.SemaphoreType.DMA
    return [
        vmem((GROUPS, LOCAL_VARS, SHARE, WIDTH), BF),
        vmem((48, WIDTH), BF),
        vmem((SHARE, WIDTH), BF),
        vmem((WIDTH, WIDTH), BF),
        vmem((16, 64), F32),
        vmem((WIDTH, WIDTH), BF),
        vmem((WIDTH, WIDTH), BF),
        vmem((1, WIDTH), F32),
        vmem((3, WIDTH, LANES), BF),
        vmem((GROUPS, 4, 2, 16, WIDTH), BF),
        vmem((1, WIDTH), F32),
        vmem((2, 4, 2, LANES, 512), BF),
        vmem((2, 4, 2, 64, WIDTH), BF),
        vmem((WIDTH, LANES), BF),
        vmem((LANES, WIDTH), BF),
        vmem((2, LANES, LANES), BF),
        vmem((2, LOCAL_VARS * SHARE, WIDTH), BF),
        vmem((2, LOCAL_VARS * SHARE, LANES), BF),
        vmem((GROUPS, SHARE, WIDTH + LANES), BF),
        vmem((GROUPS, SHARE, WIDTH + LANES), BF),
        vmem((GROUPS, SHARE, WIDTH), BF),
        vmem((2 * ROWS, LANES), BF),
        vmem((ROWS // 2, LANES), BF),
        vmem((ROWS // 2, LANES), BF),
        vmem((ROWS, LANES), BF),
        vmem((16, ROWS, LANES), BF),
        vmem((2 * ROWS, LANES), F32),
        vmem((2 * ROWS, LANES), F32),
        vmem((2, GROUPS, SHARE, LANES), BF),
        vmem((2, GROUPS, SHARE, LANES), BF),
        vmem((4, SHARE, WIDTH), BF),
        vmem((4, SHARE, LANES), BF),
        vmem((GROUPS, ROWS // 2, LANES), BF),
        vmem((GROUPS, ROWS // 2, LANES), BF),
        dma((LOADS,)),
        dma((GROUPS,)),
        dma((GROUPS,)),
        dma((GROUPS,)),
        dma((GROUPS,)),
        dma((GROUPS,)),
        dma((2,)),
        dma((1,)),
        dma((16,)),
        dma((16,)),
        dma((12,)),
        dma((12,)),
        dma((2 * GROUPS,)),
        dma((2 * GROUPS,)),
        dma((2 * GROUPS,)),
        dma((2 * GROUPS,)),
        dma((GROUPS,)),
        dma((GROUPS,)),
        dma((GROUPS,)),
        dma((GROUPS,)),
    ]


def body(
    fields,
    var_embed,
    pos_embed,
    agg_key,
    agg_query,
    agg_value,
    agg_out,
    gain_one,
    qkv_weight,
    attn_out,
    gain_two,
    mlp_in,
    mlp_out,
):
    return pl.pallas_call(
        kernel,
        out_shape=jax.ShapeDtypeStruct((ROWS, LANES), BF),
        in_specs=[pl.BlockSpec(memory_space=pl.ANY)] * 13,
        out_specs=pl.BlockSpec(memory_space=pltpu.VMEM),
        scratch_shapes=scratch(),
        compiler_params=pltpu.CompilerParams(
            collective_id=0, has_side_effects=True, vmem_limit_bytes=56 * 2**20
        ),
    )(
        fields,
        var_embed,
        pos_embed,
        agg_key,
        agg_query,
        agg_value,
        agg_out,
        gain_one.reshape(1, WIDTH),
        qkv_weight,
        attn_out.reshape(4, 2, 16, WIDTH),
        gain_two.reshape(1, WIDTH),
        mlp_in.reshape(4, 2, LANES, 512),
        mlp_out.reshape(4, 2, 64, WIDTH),
    )


def solution(mesh):
    placed = (
        P("var", "tok", None),
        P(),
        P("tok", None),
        P(),
        P(),
        P(),
        P(),
        P(),
        P(None, None, "var"),
        P("var", None),
        P(),
        P(None, "var"),
        P("var", None),
    )
    return jax.shard_map(
        body, mesh=mesh, in_specs=placed, out_specs=P("tok", "var"), check_vma=False
    )
```

```python
import functools

import jax
import jax.numpy as jnp
from jax import lax
from jax.experimental import pallas as pl
from jax.experimental.pallas import tpu as pltpu
from jax.sharding import PartitionSpec as P

EPS = 1e-05
MESH = pl.DeviceIdType.MESH
BF = jnp.bfloat16
F32 = jnp.float32
GROUPS = 8
SHARE = 48
ROWS = 384
WIDTH = 1024
LANES = 128
LOCAL_VARS = 6
LOADS = 12


def mm(a, b):
    return jnp.dot(a, b, preferred_element_type=F32)


def mm_nt(a, b):
    return lax.dot_general(a, b, (((1,), (1,)), ((), ())), preferred_element_type=F32)


def lane_of(shape):
    return lax.broadcasted_iota(jnp.int32, shape, len(shape) - 1)


def split_three(value):
    high = value.astype(BF).astype(F32)
    rest = value - high
    middle = rest.astype(BF).astype(F32)
    return high, middle, rest - middle


def layer_norm(values, gain):
    center = values - jnp.mean(values, axis=-1, keepdims=True)
    spread = jnp.mean(center * center, axis=-1, keepdims=True)
    return (center * lax.rsqrt(spread + EPS) * gain).astype(BF)


def kernel(
    fields,
    var_embed,
    pos_embed,
    agg_key,
    agg_query,
    agg_value,
    agg_out,
    gain_one,
    qkv_weight,
    attn_out,
    gain_two,
    mlp_in,
    mlp_out,
    out,
    field_s,
    embed_s,
    pos_s,
    key_s,
    query_s,
    value_s,
    aggout_s,
    gain1_s,
    qkv_s,
    attnout_s,
    gain2_s,
    mlpin_s,
    mlpout_s,
    kq_s,
    spread_s,
    pick_s,
    emb_s,
    weight_s,
    part_s,
    part_r,
    norm_r,
    q_s,
    qout_s,
    qin_r,
    kvout_s,
    kv_r,
    max_s,
    acc_s,
    att_s,
    att_r,
    upd_r,
    res_r,
    down_s,
    down_r,
    load_sem,
    field_sem,
    p1_send,
    p1_recv,
    p3_send,
    p3_recv,
    z_send,
    z_recv,
    kv_send,
    kv_recv,
    w_send,
    w_recv,
    v_send,
    v_recv,
    a_send,
    a_recv,
    p8_send,
    p8_recv,
    p10_send,
    p10_recv,
):
    tok = lax.axis_index("tok")
    me = lax.axis_index("var")
    core = lax.rem(tok, 2)
    half = tok // 8
    ring = lax.rem(tok // 2, 4)
    sibling = tok + 1 - 2 * core
    partner = tok + 8 - 16 * half

    def along_x(step):
        return half * 8 + lax.rem(ring + step, 4) * 2 + core

    plane = me // 4
    high_y = lax.rem(me, 4)

    def peer(step):
        return lax.rem(plane + 1 + step // 4, 2) * 4 + lax.rem(high_y + 3 - step % 4, 4)

    def remote(src, dst, send, recv, to_tok, to_var):
        return pltpu.make_async_remote_copy(
            src_ref=src,
            dst_ref=dst,
            send_sem=send,
            recv_sem=recv,
            device_id=(to_tok, to_var),
            device_id_type=MESH,
        )

    barrier = pltpu.get_barrier_semaphore()
    others = [(tok, peer(i)) for i in range(GROUPS - 1)]
    others += [(partner, lax.rem(me + i, GROUPS)) for i in range(GROUPS)]
    others += [(sibling, me)] + [(along_x(i), me) for i in (1, 2, 3)]
    for device in others:
        pl.semaphore_signal(barrier, inc=1, device_id=device, device_id_type=MESH)

    def field_copy(i):
        rows = pl.ds(pl.multiple_of(peer(i) * SHARE, 16), SHARE)
        return pltpu.make_async_copy(fields.at[:, rows, :], field_s.at[i], field_sem.at[i])

    own_rows = pl.ds(pl.multiple_of(me * SHARE, 16), SHARE)
    loads = [
        pltpu.make_async_copy(src, dst, load_sem.at[k])
        for k, (src, dst) in enumerate(
            [
                (agg_query, query_s),
                (var_embed, embed_s),
                (agg_key, key_s),
                (agg_value, value_s),
                (agg_out, aggout_s),
                (pos_embed.at[own_rows, :], pos_s),
                (gain_one, gain1_s),
                (qkv_weight, qkv_s),
                (attn_out.at[ring, core], attnout_s.at[me, ring, core]),
                (gain_two, gain2_s),
                (mlp_in, mlpin_s.at[0]),
                (mlp_out, mlpout_s.at[0]),
            ]
        )
    ]
    for k in (8, 0, 1, 2):
        loads[k].start()
    field_copy(0).start()
    loads[3].start()
    field_copy(1).start()

    row = lax.broadcasted_iota(jnp.int32, (LANES, WIDTH), 0)
    col = lax.broadcasted_iota(jnp.int32, (LANES, WIDTH), 1)
    spread_s[...] = jnp.where((row < 32) & (row % 16 == col // 64), 1.0, 0.0).astype(BF)
    row = lax.broadcasted_iota(jnp.int32, (LANES, LANES), 0)
    col = lax.broadcasted_iota(jnp.int32, (LANES, LANES), 1)
    same = row % 16 == col % 16
    pick_s[0] = jnp.where(same & (row < 48), 1.0, 0.0).astype(BF)
    pick_s[1] = jnp.where(same & (row >= 48) & (row < 96), 1.0, 0.0).astype(BF)

    loads[0].wait()
    heads = query_s[...]
    tiled = jnp.concatenate([heads] * 16, axis=1)
    row = lax.broadcasted_iota(jnp.int32, (16, WIDTH), 0)
    col = lax.broadcasted_iota(jnp.int32, (16, WIDTH), 1)
    tiled = jnp.where(col // 64 == row, tiled, 0.0)
    stacked = jnp.concatenate(split_three(tiled) + (jnp.zeros((80, WIDTH), F32),), axis=0)
    stacked = stacked.T.astype(BF)
    loads[2].wait()
    folded = mm(key_s[...], stacked)
    folded = folded + pltpu.roll(folded, 112, 1) + pltpu.roll(folded, 96, 1)
    folded = jnp.where(lane_of((WIDTH, LANES)) < 16, folded * 0.125, 0.0)
    for shift in (16, 32, 64):
        folded = folded + pltpu.roll(folded, shift, 1)
    kq_s[...] = folded.astype(BF)

    loads[1].wait()
    row = lax.broadcasted_iota(jnp.int32, (16, 48), 0)
    col = lax.broadcasted_iota(jnp.int32, (16, 48), 1)
    chosen = jnp.where((col == me * LOCAL_VARS + row) & (row < LOCAL_VARS), 1.0, 0.0).astype(BF)
    own_embed = mm(chosen, embed_s[...]).astype(BF)

    across = lax.rem(me + 4, GROUPS)
    mlp = (mlpin_s, mlpout_s)

    def w_copy(i, source):
        at = attnout_s.at[source, ring, core]
        return remote(at, at, w_send.at[i], w_recv.at[source], tok, peer(i))

    def mlp_copy(k):
        return remote(
            mlp[k].at[0, ring, core], mlp[k].at[1, ring, core], w_send.at[8 + k], w_recv.at[8 + k], tok, across
        )

    def spread_copy(k, step, place):
        at = attnout_s.at[:, place, core] if k == 2 else mlp[k].at[1, place, core]
        n = k * 3 + step - 1
        return remote(at, at, v_send.at[n], v_recv.at[n], along_x(step), me)

    def pair_copy(k, owner):
        at = attnout_s.at[:, :, owner] if k == 2 else mlp[k].at[1, :, owner]
        return remote(at, at, v_send.at[9 + k], v_recv.at[9 + k], sibling, me)

    def spread_arrived(k):
        for step in (1, 2, 3):
            spread_copy(k, step, lax.rem(ring + 4 - step, 4)).wait_recv()

    lane = lane_of((SHARE, LANES))

    def p1_copy(i, source):
        return remote(
            part_s.at[i], part_r.at[source], p1_send.at[i], p1_recv.at[source], tok, peer(i)
        )

    def weigh(i):
        at = i % 2
        for v in range(LOCAL_VARS):
            emb_s[at, v * SHARE : (v + 1) * SHARE, :] = field_s[i, v] + own_embed[v : v + 1, :]
        scores = mm(emb_s[at], kq_s[...]).reshape(LOCAL_VARS, SHARE, LANES)
        highest = jnp.max(scores, axis=0)
        expd = jnp.exp(scores - highest[None])
        totals = jnp.sum(expd, axis=0)
        coarse = expd.astype(BF).astype(F32)
        weights = jnp.where((lane < 16)[None], coarse, jnp.where((lane < 32)[None], expd - coarse, 0.0))
        weight_s[at] = weights.reshape(LOCAL_VARS * SHARE, LANES).astype(BF)
        high, middle, low = split_three(highest)
        high_t, middle_t, low_t = split_three(totals)
        notes = jnp.where(lane < 16, high, jnp.where(lane < 32, middle, low))
        notes_t = jnp.where(lane < 64, high_t, jnp.where(lane < 80, middle_t, low_t))
        part_s[i, :, WIDTH:] = jnp.where(lane < 48, notes, notes_t).astype(BF)

    def add_up(i):
        at = i % 2
        for n in range(2):
            cols = slice(n * 512, (n + 1) * 512)
            wide = mm(weight_s[at], spread_s[:, cols])
            projected = mm(emb_s[at], value_s[:, cols])
            term = (wide * projected).reshape(LOCAL_VARS, SHARE, 512)
            part_s[i, :, cols] = jnp.sum(term, axis=0).astype(BF)

    field_copy(0).wait()
    weigh(0)
    loads[3].wait()
    for i in range(GROUPS):
        if i + 2 < GROUPS:
            field_copy(i + 2).start()
        if i == 1:
            for k in (4, 5, 6, 7):
                loads[k].start()
        if i == 4:
            for k in (9, 10, 11):
                loads[k].start()
        if i + 1 < GROUPS:
            field_copy(i + 1).wait()
            weigh(i + 1)
        add_up(i)
        if i == 0:
            pl.semaphore_wait(barrier, len(others))
        if i < GROUPS - 1:
            p1_copy(i, me).start()
    loads[8].wait()
    for i in range(GROUPS - 1):
        w_copy(i, me).start()
    part_r[me] = part_s[GROUPS - 1]
    for i in range(GROUPS - 1):
        p1_copy(i, peer(i)).wait_recv()

    notes = part_r[:, :, WIDTH:].reshape(ROWS, LANES)
    highest = mm(notes, pick_s[0]).reshape(GROUPS, SHARE, LANES)
    totals = mm(notes, pick_s[1]).reshape(GROUPS, SHARE, LANES)
    scale = jnp.exp(highest - jnp.max(highest, axis=0)[None])
    scale = scale / jnp.sum(scale * totals, axis=0)[None]
    coarse = scale.astype(BF).astype(F32)
    scale = jnp.where((lane < 16)[None], coarse, jnp.where((lane < 32)[None], scale - coarse, 0.0))
    scale = scale.reshape(ROWS, LANES).astype(BF)
    mixed = []
    for n in range(4):
        cols = slice(n * 256, (n + 1) * 256)
        wide = mm(scale, spread_s[:, cols]).reshape(GROUPS, SHARE, 256)
        mixed.append(jnp.sum(wide * part_r[:, :, cols].astype(F32), axis=0).astype(BF))
    mixed = jnp.concatenate(mixed, axis=1)
    for k in (4, 5, 6):
        loads[k].wait()
    stream = (mm(mixed, aggout_s[...]) + pos_s[...].astype(F32)).astype(BF)
    norm_r[me] = layer_norm(stream.astype(F32), gain1_s[...])

    def gather_copy(buffer, send, recv, i, source):
        return remote(buffer.at[source], buffer.at[source], send.at[i], recv.at[source], tok, peer(i))

    for i in range(GROUPS - 1):
        gather_copy(norm_r, p3_send, p3_recv, i, me).start()
    for k in (10, 11):
        loads[k].wait()
    for k in range(2):
        mlp_copy(k).start()
    loads[7].wait()
    for i in range(GROUPS - 1):
        w_copy(i, peer(i)).wait_recv()
    for step in (1, 2, 3):
        spread_copy(2, step, ring).start()
    for i in range(GROUPS - 1):
        gather_copy(norm_r, p3_send, p3_recv, i, peer(i)).wait_recv()

    normed = norm_r[...].reshape(ROWS, WIDTH)
    keys = mm(normed, qkv_s[1])
    values = mm(normed, qkv_s[2])
    wide_lane = lane_of((ROWS, LANES))
    left = wide_lane < 64
    kv_a = jnp.where(left, keys, pltpu.roll(values, 64, 1)).astype(BF)
    kv_b = jnp.where(left, pltpu.roll(keys, 64, 1), values).astype(BF)
    first = half == 0
    kv_r[core] = jnp.where(first, kv_a, kv_b)
    kvout_s[...] = jnp.where(first, kv_b, kv_a)

    def slot(order, owner):
        return order * 2 + owner

    z_kv = remote(kvout_s, kv_r.at[slot(1, core)], z_send.at[0], kv_recv.at[slot(1, core)], partner, me)
    z_kv.start()
    hops = ((2, 3), (3, 1), (4, 2))

    def x_copy(k, order, source):
        to = slot(order, core)
        return remote(
            kv_r.at[source], kv_r.at[to], kv_send.at[k], kv_recv.at[to], along_x(hops[k % 3][1]), me
        )

    for k in range(3):
        x_copy(k, hops[k][0], slot(0, core)).start()

    def share_copy(order, owner):
        at = slot(order, owner)
        return remote(kv_r.at[at], kv_r.at[at], kv_send.at[8 + order], kv_recv.at[at], sibling, me)

    share_copy(0, core).start()
    queries = mm(normed, qkv_s[0]) * 0.125
    rolled = pltpu.roll(queries, 64, 1)
    q_a = jnp.where(left, queries, 0.0).astype(BF)
    q_b = jnp.where(left, rolled, 0.0).astype(BF)
    q_s[0:ROWS, :] = jnp.where(first, q_a, q_b)
    other = jnp.where(first, rolled, queries)
    qout_s[...] = jnp.where(
        left[: ROWS // 2], other[: ROWS // 2], pltpu.roll(other[ROWS // 2 :], 64, 1)
    ).astype(BF)
    z_q = remote(qout_s, qin_r, z_send.at[1], z_recv.at[0], partner, me)
    z_q.start()

    spread_arrived(2)
    pair_copy(2, core).start()
    max_s[...] = jnp.full(max_s.shape, -jnp.inf, F32)
    acc_s[...] = jnp.zeros(acc_s.shape, F32)
    z_kv.wait_recv()
    for k in range(3):
        x_copy(3 + k, hops[k][0] + 3, slot(1, core)).start()
    z_q.wait_recv()
    packed = qin_r[...].astype(F32)
    q_s[ROWS : ROWS + ROWS // 2, :] = jnp.where(left[: ROWS // 2], packed, 0.0).astype(BF)
    q_s[ROWS + ROWS // 2 :, :] = jnp.where(
        left[: ROWS // 2], pltpu.roll(packed, 64, 1), 0.0
    ).astype(BF)

    def pass_on(order):
        share_copy(order, core).wait_recv()
        share_copy(order, core).start()

    share_copy(1, core).start()
    pass_on(2)
    pass_on(3)
    many_left = lane_of((4 * ROWS, LANES)) < 64

    def attend_step(step, carry):
        @pl.when(step == 1)
        def _():
            pass_on(4)
            for k in range(2):
                mlp_copy(k).wait_recv()
                for hop in (1, 2, 3):
                    spread_copy(k, hop, ring).start()

        @pl.when(step == 2)
        def _():
            pass_on(5)
            pass_on(6)

        @pl.when(step == 3)
        def _():
            pass_on(7)

        for order in (2 * step, 2 * step + 1):
            share_copy(order, 1 - core).wait_recv()
        block = kv_r[pl.ds(step * 4, 4)].reshape(4 * ROWS, LANES)
        ones = jnp.where(many_left, 1.0, block.astype(F32)).astype(BF)
        logits = mm_nt(q_s[...], block)
        before = max_s[...]
        newest = jnp.maximum(before, jnp.max(logits, axis=1, keepdims=True))
        probs = jnp.exp(logits - jnp.concatenate([newest] * 12, axis=1)).astype(BF)
        acc_s[...] = acc_s[...] * jnp.exp(before - newest) + mm(probs, ones)
        max_s[...] = newest
        return carry

    lax.fori_loop(0, 4, attend_step, 0)

    acc = acc_s[...]
    turned = pltpu.roll(acc, 64, 1)
    wide_left = lane_of((2 * ROWS, LANES)) < 64
    result = jnp.where(wide_left, turned, acc) / jnp.where(wide_left, acc, turned)
    keep = wide_left == jnp.broadcast_to(first, wide_left.shape)
    att_s[...] = jnp.where(keep, result, 0.0).astype(BF).reshape(2, GROUPS, SHARE, LANES)
    att_r[half, me] = att_s[0, me]

    def att_copy(side, i, at, source):
        to = peer(i)
        return remote(
            att_s.at[side, to],
            att_r.at[at, source],
            a_send.at[side * GROUPS + i],
            a_recv.at[at * GROUPS + source],
            tok if side == 0 else partner,
            to,
        )

    for i in range(GROUPS - 1):
        att_copy(0, i, half, me).start()
        att_copy(1, i, half, me).start()
    att_copy(1, GROUPS - 1, half, me).start()

    for i in range(GROUPS - 1):
        att_copy(0, i, half, peer(i)).wait_recv()
    for i in range(GROUPS):
        att_copy(1, i, 1 - half, peer(i)).wait_recv()

    pair_copy(2, 1 - core).wait_recv()
    attended = jnp.concatenate([att_r[0, g] + att_r[1, g] for g in range(GROUPS)], axis=1)
    attn_sum = mm(attended, attnout_s[...].reshape(WIDTH, WIDTH))
    def along_y(i):
        return lax.rem(high_y + 1 + i, 4)

    def upd_copy(i, source):
        at = upd_r.at[source]
        return remote(at, at, p8_send.at[i], p8_recv.at[source], tok, plane * 4 + along_y(i))

    def res_copy(i, source):
        to = (1 - plane) * 4 + i
        cols = pl.ds(pl.multiple_of(to * LANES, LANES), LANES)
        return remote(
            upd_r.at[high_y, :, cols], res_r.at[source], p8_send.at[4 + i], p8_recv.at[4 + source], tok, to
        )

    upd_r[high_y] = (stream.astype(F32) + attn_sum).astype(BF)
    for i in range(3):
        upd_copy(i, high_y).start()
    for i in range(4):
        res_copy(i, high_y).start()
    loads[9].wait()
    for k in range(2):
        spread_arrived(k)
        pair_copy(k, core).start()
    for i in range(3):
        upd_copy(i, along_y(i)).wait_recv()

    updated = upd_r[...].reshape(ROWS // 2, WIDTH)
    normed_two = layer_norm(updated.astype(F32), gain2_s[...])
    for k in range(2):
        pair_copy(k, 1 - core).wait_recv()
    hidden = []
    for k in range(2):
        raised = mm(normed_two, mlpin_s[k].reshape(WIDTH, 512))
        hidden.append((0.5 * raised * (1.0 + lax.erf(raised * 0.7071067811865476))).astype(BF))
    hidden = jnp.concatenate(hidden, axis=1)
    down_weight = mlpout_s[...].reshape(WIDTH, WIDTH)
    for n in range(4):
        terms = mm(hidden, down_weight[:, n * 256 : (n + 1) * 256]).astype(BF)
        down_s[2 * n] = terms[:, :LANES]
        down_s[2 * n + 1] = terms[:, LANES:]

    def down_copy(i, source):
        return remote(
            down_s.at[peer(i)],
            down_r.at[source],
            p10_send.at[i],
            p10_recv.at[source],
            tok,
            peer(i),
        )

    for i in range(GROUPS - 1):
        down_copy(i, me).start()
    down_r[me] = down_s[me]
    own_cols = pl.ds(pl.multiple_of(me * LANES, LANES), LANES)
    for i in range(4):
        res_copy(i, i).wait_recv()
    for i in range(GROUPS - 1):
        down_copy(i, peer(i)).wait_recv()

    def finish_half(which, residual):
        terms = jnp.sum(down_r[pl.ds(which * 4, 4)].astype(F32), axis=0)
        rows = pl.ds(pl.multiple_of(which * (ROWS // 2), 16), ROWS // 2)
        out[rows, :] = (residual.reshape(ROWS // 2, LANES).astype(F32) + terms).astype(BF)

    finish_half(plane, upd_r[:, :, own_cols])
    finish_half(1 - plane, res_r[...])

    for i in range(GROUPS - 1):
        p1_copy(i, me).wait_send()
        gather_copy(norm_r, p3_send, p3_recv, i, me).wait_send()
        w_copy(i, me).wait_send()
        att_copy(0, i, half, me).wait_send()
        down_copy(i, me).wait_send()
    for i in range(GROUPS):
        att_copy(1, i, half, me).wait_send()
        share_copy(i, core).wait_send()
    for k in range(3):
        x_copy(k, hops[k][0], slot(0, core)).wait_send()
        x_copy(3 + k, hops[k][0] + 3, slot(1, core)).wait_send()
    z_kv.wait_send()
    z_q.wait_send()
    for i in range(3):
        upd_copy(i, high_y).wait_send()
        pair_copy(i, core).wait_send()
        for step in (1, 2, 3):
            spread_copy(i, step, ring).wait_send()
    for i in range(4):
        res_copy(i, high_y).wait_send()
    for k in range(2):
        mlp_copy(k).wait_send()


def scratch():
    vmem = pltpu.VMEM
    dma = pltpu.SemaphoreType.DMA
    return [
        vmem((GROUPS, LOCAL_VARS, SHARE, WIDTH), BF),
        vmem((48, WIDTH), BF),
        vmem((SHARE, WIDTH), BF),
        vmem((WIDTH, WIDTH), BF),
        vmem((16, 64), F32),
        vmem((WIDTH, WIDTH), BF),
        vmem((WIDTH, WIDTH), BF),
        vmem((1, WIDTH), F32),
        vmem((3, WIDTH, LANES), BF),
        vmem((GROUPS, 4, 2, 16, WIDTH), BF),
        vmem((1, WIDTH), F32),
        vmem((2, 4, 2, LANES, 512), BF),
        vmem((2, 4, 2, 64, WIDTH), BF),
        vmem((WIDTH, LANES), BF),
        vmem((LANES, WIDTH), BF),
        vmem((2, LANES, LANES), BF),
        vmem((2, LOCAL_VARS * SHARE, WIDTH), BF),
        vmem((2, LOCAL_VARS * SHARE, LANES), BF),
        vmem((GROUPS, SHARE, WIDTH + LANES), BF),
        vmem((GROUPS, SHARE, WIDTH + LANES), BF),
        vmem((GROUPS, SHARE, WIDTH), BF),
        vmem((2 * ROWS, LANES), BF),
        vmem((ROWS // 2, LANES), BF),
        vmem((ROWS // 2, LANES), BF),
        vmem((ROWS, LANES), BF),
        vmem((16, ROWS, LANES), BF),
        vmem((2 * ROWS, LANES), F32),
        vmem((2 * ROWS, LANES), F32),
        vmem((2, GROUPS, SHARE, LANES), BF),
        vmem((2, GROUPS, SHARE, LANES), BF),
        vmem((4, SHARE, WIDTH), BF),
        vmem((4, SHARE, LANES), BF),
        vmem((GROUPS, ROWS // 2, LANES), BF),
        vmem((GROUPS, ROWS // 2, LANES), BF),
        dma((LOADS,)),
        dma((GROUPS,)),
        dma((GROUPS,)),
        dma((GROUPS,)),
        dma((GROUPS,)),
        dma((GROUPS,)),
        dma((2,)),
        dma((1,)),
        dma((16,)),
        dma((16,)),
        dma((12,)),
        dma((12,)),
        dma((2 * GROUPS,)),
        dma((2 * GROUPS,)),
        dma((2 * GROUPS,)),
        dma((2 * GROUPS,)),
        dma((GROUPS,)),
        dma((GROUPS,)),
        dma((GROUPS,)),
        dma((GROUPS,)),
    ]


def body(
    fields,
    var_embed,
    pos_embed,
    agg_key,
    agg_query,
    agg_value,
    agg_out,
    gain_one,
    qkv_weight,
    attn_out,
    gain_two,
    mlp_in,
    mlp_out,
):
    return pl.pallas_call(
        kernel,
        out_shape=jax.ShapeDtypeStruct((ROWS, LANES), BF),
        in_specs=[pl.BlockSpec(memory_space=pl.ANY)] * 13,
        out_specs=pl.BlockSpec(memory_space=pltpu.VMEM),
        scratch_shapes=scratch(),
        compiler_params=pltpu.CompilerParams(
            collective_id=0, has_side_effects=True, vmem_limit_bytes=56 * 2**20
        ),
    )(
        fields,
        var_embed,
        pos_embed,
        agg_key,
        agg_query,
        agg_value,
        agg_out,
        gain_one.reshape(1, WIDTH),
        qkv_weight,
        attn_out.reshape(4, 2, 16, WIDTH),
        gain_two.reshape(1, WIDTH),
        mlp_in.reshape(4, 2, LANES, 512),
        mlp_out.reshape(4, 2, 64, WIDTH),
    )


def solution(mesh):
    placed = (
        P("var", "tok", None),
        P(),
        P("tok", None),
        P(),
        P(),
        P(),
        P(),
        P(),
        P(None, None, "var"),
        P("var", None),
        P(),
        P(None, "var"),
        P("var", None),
    )
    return jax.shard_map(
        body, mesh=mesh, in_specs=placed, out_specs=P("tok", "var"), check_vma=False
    )
```
